256 devices in a mesh: section: 2 (over z_lo), dp: 16 (over y, z_hi), tensor: 8 (over x, core).
Axes of the slice: x: 4, y: 4, z: 8 (z_hi: 4, z_lo: 2; z = z_hi * 2 + z_lo), core: 2. Of those that a mesh axis runs over, the one named last changes fastest.
Arguments:
- byte_rows: bfloat16 [2, 16, 512, 4672], P('section', 'dp', None, 'tensor'), may hold values from -1.75 to 1.75
- context: bfloat16 [2, 16, 512, 4096], P('section', 'dp', None, 'tensor'), may hold values from -1.75 to 1.75
- weight: bfloat16 [2, 4672, 4096], P('section', 'dp', 'tensor'), may hold values from -0.09375 to 0.09375
- keep_list: int32 [16, 512], P('dp'), may hold values from 0 to 511, as said below
- counts: int32 [16], P('dp'), may hold values from 128 to 512, as said below
- gate_vector: float32 [4672], P('tensor'), may hold values from -0.09375 to 0.09375
Outputs:
- section_rows: bfloat16 [2, 16, 512, 4672], P('section', 'dp', None, 'tensor')
- gate_values: bfloat16 [2, 16, 512], P('section', 'dp')
- context_grad: bfloat16 [2, 16, 512, 4096], P('section', 'dp', None, 'tensor')
- weight_grad: bfloat16 [2, 4672, 4096], P('section', 'dp', 'tensor')
The draws below stay inside these ranges and needn't reach their ends.
Inputs may be any that keep to these rules, and one draw needn't show every extreme that they name: `keep_list`: for each sequence b, entries 0 to counts[b] - 1 are distinct byte positions in increasing order; the entries after them are 0. `counts`: some sequence keeps all 512 bytes.
All inputs are finite; a program needn't handle non-finite values.
Results may differ from the reference program's by a relative error of at most 0.02.
Values may be sent and summed in bfloat16 or wider, within the bound.
A program may use at most 64 MiB of HBM per device.

```python
import jax
import jax.numpy as jnp
from jax import lax

D = 4672
INNER = 4096
SEQ_DEV = 1
LEN = 512
SEQS = 16
INNER_DEV = 512
N_DP = 16
N_TENSOR = 8


def rank_row(row_key):
    return jax.random.permutation(row_key, LEN)


def pack_lists(key):
    count_key, full_key, rank_key = jax.random.split(key, 3)
    kept = jax.random.randint(count_key, (SEQS,), LEN // 4, LEN + 1)
    chosen = jax.random.randint(full_key, (), 0, SEQS)
    kept = jnp.where(jnp.arange(SEQS) == chosen, LEN, kept).astype(jnp.int32)
    ranks = jax.vmap(rank_row)(jax.random.split(rank_key, SEQS))
    flagged = ranks < kept[:, None]
    order_score = jnp.where(flagged, 0, LEN) + jnp.arange(LEN)[None, :]
    ordered = jnp.argsort(order_score, axis=1, stable=True).astype(jnp.int32)
    live = jnp.arange(LEN)[None, :] < kept[:, None]
    keep_list = jnp.where(live, ordered, 0).astype(jnp.int32)
    return (keep_list, kept)


def draw_keep_list(key, part):
    return pack_lists(key)[0]


def draw_counts(key, part):
    return pack_lists(key)[1]


def block_scale(rng, extent, cuts, smallest, top_value):
    gain, own = 1.0, jax.random.fold_in(rng, 6)
    for axis_at, shards_of in cuts:
        draws = jnp.exp(jax.random.uniform(jax.random.fold_in(own, axis_at), (shards_of,), jnp.float32, smallest / len(cuts), top_value / len(cuts)))
        gain = gain * jnp.repeat(draws, extent[axis_at] // shards_of).reshape([-1 if axis == axis_at else 1 for axis in range(len(extent))])
    return gain


def gaussian(key, shape, width, limit, cuts=(), dtype=jnp.bfloat16):
    level = block_scale(key, shape, cuts, -0.22, 0.18) if cuts else 1.0
    entries = jax.random.normal(key, shape, jnp.float32) * width * level
    return jnp.minimum(jnp.maximum(entries, -limit), limit).astype(dtype)


def setup_inputs(seed: int = 0) -> dict:
    streams_of = jax.random.split(jax.random.key(seed), 7)
    byte_rows = gaussian(streams_of[0], (2, SEQS, LEN, D), 0.3, 1.75, ((0, 2), (1, 16), (3, 8)))
    context = gaussian(streams_of[1], (2, SEQS, LEN, INNER), 0.3, 1.75, ((0, 2), (1, 16), (3, 8)))
    weight = gaussian(streams_of[2], (2, D, INNER), INNER ** -0.5, 0.09375, ((0, 2), (1, 16), (2, 8)))
    keep_list = draw_keep_list(jax.random.fold_in(streams_of[6], 71), 0)
    counts = draw_counts(jax.random.fold_in(streams_of[6], 71), 0)
    gate_vector = gaussian(streams_of[5], (D,), D ** -0.5, 0.09375, ((0, 8),), jnp.float32)
    return {"byte_rows": byte_rows, "context": context, "weight": weight, "keep_list": keep_list, "counts": counts, "gate_vector": gate_vector}


epsilon = 1e-06
sharpness = 30.0

def project(context_part, weight_part):
    total = jnp.zeros((SEQS, LEN, D), jnp.float32)
    for block in range(N_TENSOR):
        lower = block * INNER_DEV
        term = jnp.einsum('bpi,di->bpd', context_part[:, :, lower:lower + INNER_DEV].astype(jnp.float32), weight_part[:, lower:lower + INNER_DEV].astype(jnp.float32))
        total = total + term.astype(jnp.bfloat16).astype(jnp.float32)
    return total

def weight_total(grad_part, context_part):
    total = jnp.zeros((D, INNER), jnp.float32)
    for block in range(N_DP):
        lower = block * SEQ_DEV
        term = jnp.einsum('bpd,bpi->di', grad_part[lower:lower + SEQ_DEV].astype(jnp.float32), context_part[lower:lower + SEQ_DEV].astype(jnp.float32))
        total = total + term.astype(jnp.bfloat16).astype(jnp.float32)
    return total.astype(jnp.bfloat16)

def pick_rows(table, index):
    return table[index]

def spread_rows(index, values):
    return jnp.zeros((LEN, values.shape[1]), jnp.float32).at[index].add(values)

def reference(byte_rows, context, weight, keep_list, counts, gate_vector):
    live = jnp.arange(LEN)[None, :] < counts[:, None]
    early_out = (byte_rows[0].astype(jnp.float32) + project(context[0], weight[0])).astype(jnp.bfloat16)
    hidden_wide = early_out.astype(jnp.float32)
    inverse_rms = jax.lax.rsqrt(lax.optimization_barrier(jnp.sum(hidden_wide * hidden_wide, axis=-1)) / D + epsilon)
    gate_score = inverse_rms * lax.optimization_barrier(jnp.sum(hidden_wide * gate_vector, axis=-1))
    squashed = jax.nn.sigmoid(gate_score)
    gate_value = (-sharpness * squashed).astype(jnp.bfloat16)
    packed = jax.vmap(pick_rows)(early_out, keep_list)
    packed = jnp.where(live[:, :, None], packed, jnp.zeros_like(packed))
    packed_gate = jnp.where(live, jax.vmap(pick_rows)(gate_value, keep_list), jnp.zeros_like(gate_value))
    late_wide = packed.astype(jnp.float32) + project(context[1], weight[1])
    late_out = jnp.where(live[:, :, None], late_wide, 0.0).astype(jnp.bfloat16)
    late_grad = jnp.where(live[:, :, None], byte_rows[1], jnp.zeros_like(byte_rows[1]))
    spread = jax.vmap(spread_rows)(keep_list, late_grad.astype(jnp.float32))
    score_grad = -sharpness * squashed * (1.0 - squashed)
    gate_part = score_grad[:, :, None] * (inverse_rms[:, :, None] * gate_vector - (gate_score * inverse_rms * inverse_rms / D)[:, :, None] * hidden_wide)
    early_grad = (spread + gate_part).astype(jnp.bfloat16)
    section_rows = jnp.stack([early_grad, late_out])
    gate_values = jnp.stack([gate_value, packed_gate])
    grads = [early_grad, late_grad]
    context_grad = jnp.stack([jnp.einsum('bpd,di->bpi', grads[index].astype(jnp.float32), weight[index].astype(jnp.float32)).astype(jnp.bfloat16) for index in range(2)])
    weight_grad = jnp.stack([weight_total(grads[index], context[index]) for index in range(2)])
    return (section_rows, gate_values, context_grad, weight_grad)
```

```python
import jax
import jax.numpy as jnp
from jax import lax
from jax.experimental import pallas as pl
from jax.experimental.pallas import tpu as pltpu
from jax.sharding import PartitionSpec as P

D = 4672
SLAB = 292
PAD = 304
HEAD = 160
TAIL = PAD - HEAD
LEN = 512
INNER_DEV = 512
EPSILON = 1e-06
SHARPNESS = 30.0

MESH = pl.DeviceIdType.MESH
F32 = jnp.float32
BF16 = jnp.bfloat16


def place():
    s = lax.axis_index("section")
    d = lax.axis_index("dp")
    t = lax.axis_index("tensor")
    return s, lax.div(d, 4), lax.rem(d, 4), lax.div(t, 2), lax.rem(t, 2)


def device(s, y, z, x, c):
    return (s, y * 4 + z, x * 2 + c)


def turn(i, step):
    return lax.rem(i + step, 4)


def send(src, dst, send_sem, recv_sem, to):
    return pltpu.make_async_remote_copy(
        src_ref=src,
        dst_ref=dst,
        send_sem=send_sem,
        recv_sem=recv_sem,
        device_id=to,
        device_id_type=MESH,
    )


def greet(peers):
    barrier = pltpu.get_barrier_semaphore()
    for peer in peers:
        pl.semaphore_signal(barrier, inc=1, device_id=peer, device_id_type=MESH)
    pl.semaphore_wait(barrier, len(peers))


def forward_kernel(
    w_ref, ctx_ref, byte_ref, g_ref, kcol_ref, krow_ref,
    grad_ref, e_ref, proj_ref, gate_ref, wout_ref,
    wf, part, ra, rb, xin, spread, st_out, st_in,
    ws, wr, as_, ar, bs, br, xs, ss, sr, ls,
):
    s, y, z, x, c = place()
    t = x * 2 + c
    up, down = device(s, turn(y, 1), z, x, c), device(s, turn(y, 3), z, x, c)
    right, left = device(s, y, turn(z, 1), x, c), device(s, y, turn(z, 3), x, c)
    sibling = device(s, y, z, x, 1 - c)
    partner = device(1 - s, y, z, x, c)
    team = [(s, y * 4 + z, lax.rem(t + j, 8)) for j in range(1, 8)]
    greet([up, down, right, left, partner] + team)

    started = []

    def go(copy):
        copy.start()
        started.append(copy)

    def slab(yy, zz):
        return yy * 4 + zz

    def whole(ref, k):
        return ref.at[k]

    def head(ref, k):
        return ref.at[k, pl.ds(0, HEAD)]

    def tail(ref, k):
        return ref.at[k, pl.ds(HEAD, TAIL)]

    def arrived(k):
        send(wf.at[k], wf.at[k], ws.at[0], wr.at[k, 0], up).wait_recv()

    def arrived_halves(k):
        send(head(wf, k), head(wf, k), ws.at[0], wr.at[k, 0], up).wait_recv()
        send(tail(wf, k), tail(wf, k), ws.at[0], wr.at[k, 1], up).wait_recv()

    own = slab(y, z)

    go(send(w_ref, wf.at[own], ws.at[4], wr.at[own, 0], up))
    go(send(w_ref, wf.at[own], ws.at[5], wr.at[own, 0], down))
    go(send(w_ref, wf.at[own], ws.at[0], wr.at[own, 0], right))
    go(send(w_ref, wf.at[own], ws.at[1], wr.at[own, 0], left))

    rows_out = send(byte_ref, xin, xs.at[0], xs.at[1], partner)

    @pl.when(s == 1)
    def _():
        rows_out.start()

    wf[own] = w_ref[...]

    def y_whole(zz, g):
        k = slab(y, zz)
        go(send(wf.at[k], wf.at[k], ws.at[4 + 4 * g], wr.at[k, 0], up))
        go(send(wf.at[k], wf.at[k], ws.at[5 + 4 * g], wr.at[k, 0], down))

    def y_halves(zz, g):
        below, above = slab(turn(y, 3), zz), slab(turn(y, 1), zz)
        arrived(below)
        go(send(head(wf, below), head(wf, below), ws.at[6 + 4 * g], wr.at[below, 0], up))
        arrived(above)
        go(send(tail(wf, above), tail(wf, above), ws.at[7 + 4 * g], wr.at[above, 1], down))

    def slot(yy, zz):
        return yy * 2 + lax.rem(zz, 2)

    def mine(zz):
        return lax.div(zz, 2) == c

    def to_sibling(yy, zz):
        i = slot(yy, zz)
        return send(part.at[slab(yy, zz)], ra.at[i], as_.at[i], ar.at[i], sibling)

    def to_owner(yy, zz):
        i, j = slot(yy, zz), x * 2 + lax.rem(zz, 2)
        return send(
            part.at[slab(yy, zz)], rb.at[j], bs.at[i], br.at[j], device(s, y, z, yy, c)
        )

    def project(yy, zz):
        k = slab(yy, zz)
        part[k] = lax.dot_general(
            wf[k], ctx_ref[...], (((1,), (1,)), ((), ())), preferred_element_type=F32
        ).astype(BF16)

        @pl.when(jnp.logical_not(mine(zz)))
        def _():
            to_sibling(yy, zz).start()

    def collect(yy, zz):
        @pl.when(mine(zz))
        def _():
            k = slab(yy, zz)
            to_sibling(yy, zz).wait_recv()
            part[k] = (part[k].astype(F32) + ra[slot(yy, zz)].astype(F32)).astype(BF16)

            @pl.when(yy != x)
            def _():
                to_owner(yy, zz).start()

    def work(count, pick):
        if count == 1:
            project(*pick(0))
            collect(*pick(0))
            return

        @pl.loop(0, count)
        def _(i):
            project(*pick(i))

        @pl.loop(0, count)
        def _(i):
            collect(*pick(i))

    z2 = turn(z, 2)
    y2 = turn(y, 2)

    def beside(zz):
        return lambda i: (turn(y, 1 + 2 * i), zz)

    work(1, lambda i: (y, z))
    y_halves(z, 0)
    work(2, beside(z))
    arrived_halves(slab(y2, z))
    work(1, lambda i: (y2, z))

    zr, zl = turn(z, 1), turn(z, 3)
    arrived(slab(y, zl))
    go(send(head(wf, slab(y, zl)), head(wf, slab(y, zl)), ws.at[2], wr.at[slab(y, zl), 0], right))
    y_whole(zl, 1)
    arrived(slab(y, zr))
    go(send(tail(wf, slab(y, zr)), tail(wf, slab(y, zr)), ws.at[3], wr.at[slab(y, zr), 1], left))
    y_whole(zr, 2)
    work(2, lambda i: (y, turn(z, 3 - 2 * i)))

    place_of = lax.broadcasted_iota(jnp.int32, (LEN, LEN), 1)

    @pl.when(s == 0)
    def _():
        rows_out.wait_recv()
        pick = jnp.where(kcol_ref[...] == place_of, 1.0, 0.0).astype(BF16)
        for i in range(2):
            spread[i] = jnp.dot(xin[i], pick, preferred_element_type=F32).astype(BF16)

    y_halves(zl, 1)
    arrived_halves(slab(y, z2))
    y_whole(z2, 3)
    work(2, beside(zl))
    work(1, lambda i: (y, z2))
    y_halves(zr, 2)
    work(2, beside(zr))
    arrived_halves(slab(y2, zl))
    arrived_halves(slab(y2, zr))
    work(2, lambda i: (y2, turn(z, 3 - 2 * i)))
    y_halves(z2, 3)
    work(2, beside(z2))
    arrived_halves(slab(y2, z2))
    keep_weight = pltpu.make_async_copy(wf, wout_ref, ls.at[0])
    keep_weight.start()
    work(1, lambda i: (y2, z2))

    def total_of(i):
        total = part[t * 2 + i].astype(F32)
        for step in range(1, 4):
            j = turn(x, step) * 2 + i
            send(rb.at[j], rb.at[j], bs.at[0], br.at[j], up).wait_recv()
            total = total + rb[j].astype(F32)
        return total

    @pl.when(s == 0)
    def _():
        st_out[...] = jnp.zeros_like(st_out)
        for i in range(2):
            e = (byte_ref[i].astype(F32) + total_of(i)).astype(BF16)
            e_ref[i] = e
            e = e.astype(F32)
            st_out[0:1] += jnp.sum(e * e, axis=0, keepdims=True)
            st_out[1:2] += jnp.sum(e * g_ref[i], axis=0, keepdims=True)
        st_in[t] = st_out[...]
        stats = [
            send(st_out, st_in.at[t], ss.at[j], sr.at[j], peer) for j, peer in enumerate(team)
        ]
        for copy in stats:
            copy.start()
        for copy in stats:
            copy.wait()
        sums = st_in[0]
        for j in range(1, 8):
            sums = sums + st_in[j]
        inverse = lax.rsqrt(sums[0:1] / D + EPSILON)
        score = inverse * sums[1:2]
        squashed = jax.nn.sigmoid(score)
        gate = (-SHARPNESS * squashed).astype(BF16)
        gate_ref[...] = jnp.broadcast_to(gate, gate_ref.shape)
        slope = -SHARPNESS * squashed * (1.0 - squashed)
        pull = score * inverse * inverse / D
        for i in range(2):
            gate_part = slope * (inverse * g_ref[i] - pull * e_ref[i].astype(F32))
            grad_ref[i] = (spread[i].astype(F32) + gate_part).astype(BF16)

    @pl.when(s == 1)
    def _():
        live = krow_ref[...] >= 0
        for i in range(2):
            proj_ref[i] = total_of(i)
            rows = byte_ref[i]
            grad_ref[i] = jnp.where(live, rows, jnp.zeros_like(rows))
        rows_out.wait_send()

    for copy in started:
        copy.wait_send()

    @pl.loop(0, 16)
    def _(k):
        yy, zz = lax.div(k, 4), lax.rem(k, 4)

        @pl.when(jnp.logical_not(mine(zz)))
        def _():
            to_sibling(yy, zz).wait_send()

        @pl.when(jnp.logical_and(mine(zz), yy != x))
        def _():
            to_owner(yy, zz).wait_send()

    keep_weight.wait()


def backward_kernel(
    grad_ref, e_ref, proj_ref, gate_ref, w_ref, ctx_ref, krow_ref,
    rows_ref, gout_ref, cgrad_ref, wgrad_ref,
    gf, wf, wp, yh, yr, ysum, zh, zr, xin, gin, cacc, last,
    gs, gr, hs, hr, fs, fr, zs, zrs, xs, ls,
):
    s, y, z, x, c = place()
    t = x * 2 + c
    up, down = device(s, turn(y, 1), z, x, c), device(s, turn(y, 3), z, x, c)
    right, left = device(s, y, turn(z, 1), x, c), device(s, y, turn(z, 3), x, c)
    east, west = device(s, y, z, turn(x, 1), c), device(s, y, z, turn(x, 3), c)
    sibling = device(s, y, z, x, 1 - c)
    partner = device(1 - s, y, z, x, c)
    load = pltpu.make_async_copy(w_ref, wf, ls.at[0])
    load.start()
    greet([up, down, right, left, east, west, sibling, partner])

    started = []

    def go(copy):
        copy.start()
        started.append(copy)

    def pass_on(k, i, to):
        go(send(gf.at[k], gf.at[k], gs.at[i], gr.at[k], to))

    def arrived(k):
        send(gf.at[k], gf.at[k], gs.at[0], gr.at[k], east).wait_recv()

    for i in range(2):
        k = t * 2 + i
        go(send(grad_ref.at[i], gf.at[k], gs.at[i], gr.at[k], east))
        go(send(grad_ref.at[i], gf.at[k], gs.at[2 + i], gr.at[k], west))
        go(send(grad_ref.at[i], gf.at[k], gs.at[4 + i], gr.at[k], sibling))
        gf[k] = grad_ref[i]

    rows_out = send(e_ref, xin, xs.at[0], xs.at[1], partner)
    gate_out = send(gate_ref, gin, xs.at[2], xs.at[3], partner)

    @pl.when(s == 0)
    def _():
        rows_out.start()
        gate_out.start()

    def halves(yy, zz):
        k = yy * 4 + zz
        return (
            send(wp.at[k, pl.ds(0, HEAD)], yh.at[0, zz], hs.at[0, zz], hr.at[0, zz], up),
            send(
                wp.at[k, pl.ds(HEAD, TAIL)], yh.at[1, zz, pl.ds(0, TAIL)],
                hs.at[1, zz], hr.at[1, zz], down,
            ),
        )

    def one_way(yy, zz, way, to):
        return send(wp.at[yy * 4 + zz], yr.at[way, zz], fs.at[way, zz], fr.at[way, zz], to)

    order = (2, 1, 3, 0)

    def compute(step):
        yy = turn(x, step)
        far = lax.rem(yy - y + 4, 4) == 2

        @pl.loop(0, 4)
        def _(i):
            zz = turn(z, i)
            k = yy * 4 + zz

            @pl.when(jnp.logical_and(lax.div(zz, 2) != c, True))
            def _():
                arrived(k)

            wp[k] = jnp.dot(gf[k], ctx_ref[...], preferred_element_type=F32).astype(BF16)

            @pl.when(far)
            def _():
                for copy in halves(yy, zz):
                    copy.start()

    def forward(step):
        yy = turn(x, step)
        rel = lax.rem(yy - y + 4, 4)
        for off in order:
            zz = turn(z, off)
            k = yy * 4 + zz
            to_head, to_tail = halves(yy, zz)

            @pl.when(rel == 1)
            def _():
                to_head.wait_recv()
                rows = pl.ds(0, HEAD)
                wp[k, rows] = (wp[k, rows].astype(F32) + yh[0, zz].astype(F32)).astype(BF16)
                one_way(yy, zz, 0, up).start()

            @pl.when(rel == 3)
            def _():
                to_tail.wait_recv()
                rows = pl.ds(HEAD, TAIL)
                wp[k, rows] = (
                    wp[k, rows].astype(F32) + yh[1, zz, pl.ds(0, TAIL)].astype(F32)
                ).astype(BF16)
                one_way(yy, zz, 1, down).start()

    def context_part(step):
        yy = turn(x, step)

        @pl.loop(0, 4)
        def _(i):
            k = yy * 4 + i
            cacc[...] += lax.dot_general(
                gf[k], wf[k], (((0,), (0,)), ((), ())), preferred_element_type=F32
            )

    cacc[...] = jnp.zeros_like(cacc)
    compute(0)
    xe, xw, xo = turn(x, 1), turn(x, 3), turn(x, 2)

    def from_west(i):
        k = (xw * 2 + c) * 2 + i
        arrived(k)
        if i == 0:
            pass_on(k, 6, east)
        pass_on(k, 8 + i, sibling)

    def from_east(i):
        k = (xe * 2 + c) * 2 + i
        arrived(k)
        if i == 1:
            pass_on(k, 7, west)
        pass_on(k, 10 + i, sibling)

    load.wait()
    context_part(0)
    from_west(0)
    from_east(0)
    from_west(1)
    from_east(1)
    forward(0)
    compute(1)
    compute(3)
    for i in range(2):
        k = (xo * 2 + c) * 2 + i
        arrived(k)
        pass_on(k, 12 + i, sibling)
    compute(2)
    context_part(1)
    forward(1)
    context_part(3)
    forward(3)
    forward(2)
    context_part(2)
    cgrad_ref[...] = cacc[...].astype(BF16)

    for off in order:
        zz = turn(z, off)
        k = y * 4 + zz
        one_way(y, zz, 0, up).wait_recv()
        one_way(y, zz, 1, down).wait_recv()
        total = wp[k].astype(F32) + yr[0, zz].astype(F32) + yr[1, zz].astype(F32)
        if off == 2:
            ysum[0] = total.astype(BF16)
            go(send(ysum.at[0, pl.ds(0, HEAD)], zh.at[0], zs.at[0], zrs.at[0], right))
            go(
                send(
                    ysum.at[0, pl.ds(HEAD, TAIL)], zh.at[1, pl.ds(0, TAIL)],
                    zs.at[1], zrs.at[1], left,
                )
            )
        elif off == 1:
            started[-2].wait_recv()
            ysum[1] = total.astype(BF16)
            rows = pl.ds(0, HEAD)
            ysum[1, rows] = (total[:HEAD] + zh[0].astype(F32)).astype(BF16)
            go(send(ysum.at[1], zr.at[0], zs.at[2], zrs.at[2], right))
        elif off == 3:
            started[-2].wait_recv()
            ysum[2] = total.astype(BF16)
            rows = pl.ds(HEAD, TAIL)
            ysum[2, rows] = (total[HEAD:] + zh[1, pl.ds(0, TAIL)].astype(F32)).astype(BF16)
            go(send(ysum.at[2], zr.at[1], zs.at[3], zrs.at[3], left))
        else:
            last[...] = total

    started[-2].wait_recv()
    started[-1].wait_recv()
    wgrad_ref[...] = (last[...] + zr[0].astype(F32) + zr[1].astype(F32)).astype(BF16)

    @pl.when(s == 0)
    def _():
        rows_ref[...] = grad_ref[...]
        gout_ref[...] = gate_ref[...]
        rows_out.wait_send()
        gate_out.wait_send()

    @pl.when(s == 1)
    def _():
        rows_out.wait_recv()
        gate_out.wait_recv()
        live = krow_ref[...] >= 0
        place_of = lax.broadcasted_iota(jnp.int32, (LEN, LEN), 0)
        pick = jnp.where(krow_ref[...] == place_of, 1.0, 0.0).astype(BF16)
        for i in range(2):
            packed = jnp.dot(xin[i], pick, preferred_element_type=F32)
            rows_ref[i] = jnp.where(live, packed + proj_ref[i], 0.0).astype(BF16)
        gout_ref[...] = jnp.dot(gin[...], pick, preferred_element_type=F32).astype(BF16)

    for copy in started:
        copy.wait_send()

    @pl.loop(0, 4)
    def _(zz):
        for copy in halves(turn(y, 2), zz):
            copy.wait_send()
        one_way(turn(y, 1), zz, 0, up).wait_send()
        one_way(turn(y, 3), zz, 1, down).wait_send()


VMEM = pl.BlockSpec(memory_space=pltpu.VMEM)
ANY = pl.BlockSpec(memory_space=pl.ANY)
LIMIT = 56 * 2**20


def forward_call(*operands):
    dma = pltpu.SemaphoreType.DMA
    return pl.pallas_call(
        forward_kernel,
        name="forward",
        out_shape=(
            jax.ShapeDtypeStruct((2, PAD, LEN), BF16),
            jax.ShapeDtypeStruct((2, PAD, LEN), BF16),
            jax.ShapeDtypeStruct((2, PAD, LEN), F32),
            jax.ShapeDtypeStruct((16, LEN), BF16),
            jax.ShapeDtypeStruct((16, PAD, INNER_DEV), BF16),
        ),
        in_specs=[VMEM] * 6,
        out_specs=(VMEM, VMEM, VMEM, VMEM, ANY),
        scratch_shapes=[
            pltpu.VMEM((16, PAD, INNER_DEV), BF16),
            pltpu.VMEM((16, PAD, LEN), BF16),
            pltpu.VMEM((8, PAD, LEN), BF16),
            pltpu.VMEM((8, PAD, LEN), BF16),
            pltpu.VMEM((2, PAD, LEN), BF16),
            pltpu.VMEM((2, PAD, LEN), BF16),
            pltpu.VMEM((8, LEN), F32),
            pltpu.VMEM((8, 8, LEN), F32),
            dma((20,)), dma((16, 2)), dma((8,)), dma((8,)), dma((8,)), dma((8,)),
            dma((2,)), dma((7,)), dma((7,)), dma((1,)),
        ],
        compiler_params=pltpu.CompilerParams(
            collective_id=0, has_side_effects=True, vmem_limit_bytes=LIMIT
        ),
    )(*operands)


def backward_call(*operands):
    dma = pltpu.SemaphoreType.DMA
    return pl.pallas_call(
        backward_kernel,
        name="backward",
        out_shape=(
            jax.ShapeDtypeStruct((2, PAD, LEN), BF16),
            jax.ShapeDtypeStruct((16, LEN), BF16),
            jax.ShapeDtypeStruct((LEN, INNER_DEV), BF16),
            jax.ShapeDtypeStruct((PAD, INNER_DEV), BF16),
        ),
        in_specs=[VMEM, VMEM, VMEM, VMEM, ANY, VMEM, VMEM],
        out_specs=(VMEM,) * 4,
        scratch_shapes=[
            pltpu.VMEM((16, PAD, LEN), BF16),
            pltpu.VMEM((16, PAD, INNER_DEV), BF16),
            pltpu.VMEM((16, PAD, INNER_DEV), BF16),
            pltpu.VMEM((2, 4, HEAD, INNER_DEV), BF16),
            pltpu.VMEM((2, 4, PAD, INNER_DEV), BF16),
            pltpu.VMEM((3, PAD, INNER_DEV), BF16),
            pltpu.VMEM((2, HEAD, INNER_DEV), BF16),
            pltpu.VMEM((2, PAD, INNER_DEV), BF16),
            pltpu.VMEM((2, PAD, LEN), BF16),
            pltpu.VMEM((16, LEN), BF16),
            pltpu.VMEM((LEN, INNER_DEV), F32),
            pltpu.VMEM((PAD, INNER_DEV), F32),
            dma((14,)), dma((16,)), dma((2, 4)), dma((2, 4)), dma((2, 4)), dma((2, 4)),
            dma((4,)), dma((4,)), dma((4,)), dma((1,)),
        ],
        compiler_params=pltpu.CompilerParams(
            collective_id=1, has_side_effects=True, vmem_limit_bytes=LIMIT
        ),
    )(*operands)


def per_device(byte_rows, context, weight, keep_list, counts, gate_vector):
    context_rows = context[0, 0]
    kept = jnp.where(lax.broadcasted_iota(jnp.int32, (1, LEN), 1) < counts[:, None], keep_list, -1)
    pad = ((0, 0), (0, PAD - SLAB), (0, 0))
    byte_slabs = jnp.pad(byte_rows[0, 0].T.reshape(2, SLAB, LEN), pad)
    gate_column = jnp.pad(gate_vector.reshape(2, SLAB, 1), pad)
    weight_rows = jnp.pad(weight[0], pad[1:])
    grad, e, proj, gate, weight_full = forward_call(
        weight_rows, context_rows, byte_slabs, gate_column, kept.reshape(LEN, 1), kept
    )
    rows, gate_out, context_grad, weight_grad = backward_call(
        grad, e, proj, gate, weight_full, context_rows, kept
    )
    section_rows = rows[:, :SLAB].reshape(2 * SLAB, LEN).T[None, None]
    return (
        section_rows,
        gate_out[0:1][None],
        context_grad[None, None],
        weight_grad[None, :SLAB],
    )


def solution(mesh):
    placed = (
        P("section", "dp", None, "tensor"),
        P("section", "dp", None, "tensor"),
        P("section", "dp", "tensor"),
        P("dp", None),
        P("dp"),
        P("tensor"),
    )
    return jax.shard_map(
        per_device,
        mesh=mesh,
        in_specs=placed,
        out_specs=(
            P("section", "dp", None, "tensor"),
            P("section", "dp", None),
            P("section", "dp", None, "tensor"),
            P("section", "dp", "tensor"),
        ),
        check_vma=False,
    )
```

```python
import jax
import jax.numpy as jnp
from jax import lax
from jax.experimental import pallas as pl
from jax.experimental.pallas import tpu as pltpu
from jax.sharding import PartitionSpec as P

D = 4672
SLAB = 292
PAD = 304
COLS = 2 * SLAB
LEN = 512
INNER_DEV = 512
EPSILON = 1e-06
SHARPNESS = 30.0

MESH = pl.DeviceIdType.MESH
F32 = jnp.float32
BF16 = jnp.bfloat16


def turn(i, step):
    return lax.rem(i + step, 4)


def send(src, dst, send_sem, recv_sem, to):
    return pltpu.make_async_remote_copy(
        src_ref=src,
        dst_ref=dst,
        send_sem=send_sem,
        recv_sem=recv_sem,
        device_id=to,
        device_id_type=MESH,
    )


def contract(a, b, axis_a, axis_b):
    return lax.dot_general(
        a, b, (((axis_a,), (axis_b,)), ((), ())), preferred_element_type=F32
    )


def kernel(
    byte_ref, ctx_ref, w_ref, keep_ref, counts_ref, g_ref,
    rows_ref, gates_ref, cgrad_ref, wgrad_ref,
    stage, wf, cf, bt, gcol, pacc, spread, e_ref, gt, st_out, st_in, gate_out, gate_in, xin,
    wp, yh, yr, zh, zr, base, final, wg, q, qa, qb,
    ws, wr, ps, pr, cs_, cr, xs, ss, sr, hs, hr, fs, fr, zs, zrs, qs, qr, os_, or_, ready,
):
    s = lax.axis_index("section")
    d = lax.axis_index("dp")
    t = lax.axis_index("tensor")
    y, z, x, c = lax.div(d, 4), lax.rem(d, 4), lax.div(t, 2), lax.rem(t, 2)

    def device(yy, zz, xx, cc):
        return (s, yy * 4 + zz, xx * 2 + cc)

    up, down = device(turn(y, 1), z, x, c), device(turn(y, 3), z, x, c)
    right, left = device(y, turn(z, 1), x, c), device(y, turn(z, 3), x, c)
    east, west = device(y, z, turn(x, 1), c), device(y, z, turn(x, 3), c)
    sibling = device(y, z, x, 1 - c)
    partner = (1 - s, d, t)
    team = [(s, d, lax.rem(t + j, 8)) for j in range(1, 8)]
    holder = device(x, z, y, lax.div(z, 2))
    owns = lax.div(z, 2) == c
    diagonal = x == y
    stays = jnp.logical_and(diagonal, owns)

    barrier = pltpu.get_barrier_semaphore()
    hello = [up, down, right, left, partner] + team
    for peer in hello:
        pl.semaphore_signal(barrier, inc=1, device_id=peer, device_id_type=MESH)

    @pl.when(jnp.logical_not(stays))
    def _():
        pl.semaphore_signal(barrier, inc=1, device_id=holder, device_id_type=MESH)

    for core in range(2):
        @pl.when(jnp.logical_and(owns, jnp.logical_not(jnp.logical_and(diagonal, c == core))))
        def _():
            pl.semaphore_signal(
                barrier, inc=1, device_id=device(x, z, y, core), device_id_type=MESH
            )

    stage[pl.ds(PAD - 16, 16)] = jnp.zeros((16, INNER_DEV), BF16)
    stage[pl.ds(0, SLAB)] = w_ref[0]
    cf[t] = ctx_ref[0, 0]
    fold = []
    for i in range(2):
        row = lax.broadcasted_iota(jnp.int32, (PAD, COLS), 0)
        col = lax.broadcasted_iota(jnp.int32, (PAD, COLS), 1)
        hit = jnp.logical_and(col == row + i * SLAB, row < SLAB)
        fold.append(jnp.where(hit, 1.0, 0.0).astype(BF16))
    for i in range(2):
        bt[i] = contract(fold[i], byte_ref[0, 0], 1, 1).astype(BF16)

    greeted = (
        len(hello)
        + jnp.where(stays, 0, 1)
        + jnp.where(owns, jnp.where(diagonal, 1, 2), 0)
    )
    pl.semaphore_wait(barrier, greeted)

    def unit(yy, zz):
        return yy * 4 + zz * 2

    def pair(ref, n):
        return ref.at[pl.ds(n, 2)]

    always = []

    def go(copy):
        copy.start()
        always.append(copy)

    def start(copies):
        for copy in copies:
            copy.start()

    home = x * 4 + lax.rem(z, 2) * 2 + c
    to_holder = send(stage, wf.at[home], ps.at[2], wr.at[home], holder)

    @pl.when(stays)
    def _():
        wf[home] = stage[...]

    @pl.when(jnp.logical_not(stays))
    def _():
        to_holder.start()

    rows_in = send(bt, xin, xs.at[0], xs.at[1], partner)
    rows_back = send(e_ref, xin, xs.at[0], xs.at[1], partner)
    gates_back = send(gate_out, gate_in, xs.at[2], xs.at[3], partner)

    @pl.when(s == 1)
    def _():
        rows_in.start()

    odd = lax.rem(z, 2)
    zz1 = jnp.where(owns, odd, 1 - odd)
    zz2 = 1 - zz1
    near = 1 - odd
    from_left = owns == (odd == 1)
    half = LEN // 2

    def context_out():
        for i, to in enumerate((east, west, sibling)):
            go(send(ctx_ref.at[0, 0], cf.at[t], cs_.at[i], cr.at[t, 0], to))

    def wait_context(it, part):
        rows = cf.at[it]
        if part is not None:
            rows = cf.at[it, pl.ds(part * half, half)]
        send(rows, rows, cs_.at[0], cr.at[it, part or 0], east).wait_recv()

    def context_on():
        for i, (xx, to) in enumerate(((turn(x, 3), east), (turn(x, 1), west))):
            it = xx * 2 + c
            wait_context(it, None)
            rows = cf.at[it, pl.ds(i * half, half)]
            go(send(rows, rows, cs_.at[3 + i], cr.at[it, i], to))
            go(send(cf.at[it], cf.at[it], cs_.at[5 + i], cr.at[it, 0], sibling))

    def context_last():
        it = turn(x, 2) * 2 + c
        wait_context(it, 0)
        wait_context(it, 1)
        go(send(cf.at[it], cf.at[it], cs_.at[7], cr.at[it, 0], sibling))
        for xx in range(4):
            wait_context(xx * 2 + 1 - c, None)

    def arrived(n):
        send(pair(wf, n), pair(wf, n), ws.at[0], wr.at[n], up).wait_recv()

    def arrived_block(n):
        send(wf.at[n], wf.at[n], ws.at[0], wr.at[n], up).wait_recv()

    def along_y(zz, u):
        n = unit(y, zz)
        return (
            send(pair(wf, n), pair(wf, n), ws.at[4 + 4 * u], wr.at[n], up),
            send(pair(wf, n), pair(wf, n), ws.at[5 + 4 * u], wr.at[n], down),
        )

    def beyond_y(zz, u):
        n, m = unit(turn(y, 3), zz), unit(turn(y, 1), zz) + 1
        return (
            send(wf.at[n], wf.at[n], ws.at[6 + 4 * u], wr.at[n], up),
            send(wf.at[m], wf.at[m], ws.at[7 + 4 * u], wr.at[m], down),
        )

    def on_along_y(zz, u):
        ahead, back = beyond_y(zz, u)
        arrived(unit(turn(y, 3), zz))
        ahead.start()
        arrived(unit(turn(y, 1), zz))
        back.start()

    def along_z():
        n = unit(y, odd)
        return (
            send(pair(wf, n), pair(wf, n), ws.at[1], wr.at[n], right),
            send(pair(wf, n), pair(wf, n), ws.at[2], wr.at[n], left),
        )

    def arrived_far(yy, zz):
        n = unit(yy, zz)
        arrived_block(n)
        arrived_block(n + 1)

    onward = (
        send(wf.at[unit(y, near)], wf.at[unit(y, near)], ws.at[3], wr.at[unit(y, near)], right),
        send(
            wf.at[unit(y, near) + 1], wf.at[unit(y, near) + 1],
            ws.at[3], wr.at[unit(y, near) + 1], left,
        ),
    )

    def on_along_z():
        arrived(unit(y, near))

        @pl.when(from_left)
        def _():
            onward[0].start()

        @pl.when(jnp.logical_not(from_left))
        def _():
            onward[1].start()

    def project(yy, zz):
        n = unit(yy, zz)
        pacc[zz] += contract(wf[n], cf[yy * 2], 1, 1) + contract(wf[n + 1], cf[yy * 2 + 1], 1, 1)

    pacc[...] = jnp.zeros_like(pacc)

    @pl.when(owns)
    def _():
        for core in range(2):
            @pl.when(jnp.logical_not(jnp.logical_and(diagonal, c == core)))
            def _():
                arrived_block(unit(y, zz1) + core)
        start(along_z())
        start(along_y(zz1, 0))
        pl.semaphore_signal(ready, inc=1, device_id=sibling, device_id_type=MESH)

    @pl.when(jnp.logical_not(owns))
    def _():
        pl.semaphore_wait(ready, 1)

    context_out()

    @pl.when(owns)
    def _():
        on_along_y(zz1, 0)
        on_along_z()
        start(along_y(zz2, 1))

    @pl.when(jnp.logical_not(owns))
    def _():
        on_along_z()
        start(along_y(zz1, 0))

    context_on()

    @pl.when(jnp.logical_not(owns))
    def _():
        arrived_far(y, zz2)
        start(along_y(zz2, 1))

    context_last()

    pick = jnp.where(
        lax.broadcasted_iota(jnp.int32, (1, LEN), 1) < counts_ref[0], keep_ref[...], -1
    )
    live = pick >= 0
    place_of = lax.broadcasted_iota(jnp.int32, (LEN, LEN), 0)
    picks = jnp.where(pick == place_of, 1.0, 0.0).astype(BF16)

    project(y, zz1)
    project(y, zz2)

    @pl.when(owns)
    def _():
        arrived_far(turn(y, 2), zz1)

    @pl.when(jnp.logical_not(owns))
    def _():
        on_along_y(zz1, 0)

    project(turn(y, 1), zz1)
    project(turn(y, 3), zz1)

    @pl.when(owns)
    def _():
        on_along_y(zz2, 1)

    @pl.when(jnp.logical_not(owns))
    def _():
        on_along_y(zz2, 1)
        arrived_far(turn(y, 2), zz1)

    @pl.when(s == 0)
    def _():
        rows_in.wait_recv()
        for i in range(2):
            spread[i] = contract(xin[i], picks, 1, 1).astype(BF16)

    g = g_ref[...]
    first = g.astype(BF16)
    rest = g - first.astype(F32)
    second = rest.astype(BF16)
    third = (rest - second.astype(F32)).astype(BF16)
    for i in range(2):
        terms = [contract(fold[i], jnp.broadcast_to(v, (16, COLS)), 1, 1) for v in (first, second, third)]
        gcol[i] = (terms[0] + terms[1] + terms[2])[:, 0:1]

    project(turn(y, 1), zz2)
    project(turn(y, 3), zz2)
    project(turn(y, 2), zz1)
    arrived_far(turn(y, 2), zz2)
    project(turn(y, 2), zz2)

    @pl.when(s == 0)
    def _():
        st_out[...] = jnp.zeros_like(st_out)
        for i in range(2):
            e = (bt[i].astype(F32) + pacc[i]).astype(BF16)
            e_ref[i] = e
            e = e.astype(F32)
            st_out[0:1] += jnp.sum(e * e, axis=0, keepdims=True)
            st_out[1:2] += jnp.sum(e * gcol[i], axis=0, keepdims=True)
        st_in[t] = st_out[...]
        stats = [
            send(st_out, st_in.at[t], ss.at[j], sr.at[j], peer) for j, peer in enumerate(team)
        ]
        for copy in stats:
            copy.start()
        rows_back.start()
        for copy in stats:
            copy.wait()
        sums = st_in[0]
        for j in range(1, 8):
            sums = sums + st_in[j]
        inverse = lax.rsqrt(sums[0:1] / D + EPSILON)
        score = inverse * sums[1:2]
        squashed = jax.nn.sigmoid(score)
        gate = (-SHARPNESS * squashed).astype(BF16)
        gate_out[...] = jnp.broadcast_to(gate, gate_out.shape)
        gates_back.start()
        slope = -SHARPNESS * squashed * (1.0 - squashed)
        pull = score * inverse * inverse / D
        for i in range(2):
            gate_part = slope * (inverse * gcol[i] - pull * e_ref[i].astype(F32))
            gt[i] = (spread[i].astype(F32) + gate_part).astype(BF16)

    @pl.when(s == 1)
    def _():
        for i in range(2):
            rows = bt[i]
            gt[i] = jnp.where(live, rows, jnp.zeros_like(rows))

    zza = jnp.where(owns, near, odd)
    zzb = 1 - zza

    def products(yy, zz):
        n = unit(yy, zz)
        for core in range(2):
            wp[n + core] = jnp.dot(
                gt[zz], cf[yy * 2 + core], preferred_element_type=F32
            ).astype(BF16)

    def halves(zz):
        n = unit(turn(y, 2), zz)
        return (
            send(wp.at[n], yh.at[0, zz], hs.at[0, zz], hr.at[0, zz], up),
            send(wp.at[n + 1], yh.at[1, zz], hs.at[1, zz], hr.at[1, zz], down),
        )

    def ways(zz):
        return (
            send(pair(wp, unit(turn(y, 1), zz)), yr.at[0, zz], fs.at[0, zz], fr.at[0, zz], up),
            send(pair(wp, unit(turn(y, 3), zz)), yr.at[1, zz], fs.at[1, zz], fr.at[1, zz], down),
        )

    def merge(zz):
        to_up, to_down = halves(zz)
        on_up, on_down = ways(zz)
        n = unit(turn(y, 1), zz)
        to_up.wait_recv()
        wp[n] = (wp[n].astype(F32) + yh[0, zz].astype(F32)).astype(BF16)
        on_up.start()
        n = unit(turn(y, 3), zz) + 1
        to_down.wait_recv()
        wp[n] = (wp[n].astype(F32) + yh[1, zz].astype(F32)).astype(BF16)
        on_down.start()

    products(turn(y, 2), zza)
    start(halves(zza))
    products(turn(y, 2), zzb)
    start(halves(zzb))
    products(turn(y, 1), zza)
    products(turn(y, 3), zza)
    merge(zza)
    products(turn(y, 1), zzb)
    products(turn(y, 3), zzb)
    merge(zzb)
    products(y, zza)
    products(y, zzb)

    def to_sibling(xx):
        return send(q.at[xx * 2 + 1 - c], qa.at[xx], qs.at[xx], qr.at[xx], sibling)

    def to_column(xx):
        return send(q.at[xx * 2 + c], qb.at[x], os_.at[xx], or_.at[x], device(y, z, xx, c))

    def context_part(it):
        n = lax.div(it, 2) * 4 + lax.rem(it, 2)
        return contract(gt[0], wf[n], 0, 0) + contract(gt[1], wf[n + 2], 0, 0)

    @pl.loop(0, 4)
    def _(j):
        xx = turn(x, j + 1)
        q[xx * 2 + 1 - c] = context_part(xx * 2 + 1 - c).astype(BF16)
        to_sibling(xx).start()

    @pl.loop(0, 4)
    def _(j):
        xx = turn(x, j + 1)
        part = context_part(xx * 2 + c)
        to_sibling(xx).wait_recv()
        q[xx * 2 + c] = (part + qa[xx].astype(F32)).astype(BF16)

        @pl.when(j < 3)
        def _():
            to_column(xx).start()

    def summed(zz, core):
        n = unit(y, zz) + core
        return wp[n].astype(F32) + yr[0, zz, core].astype(F32) + yr[1, zz, core].astype(F32)

    def wait_ways(zz):
        for copy in ways(zz):
            copy.wait_recv()

    far_z = (
        send(base.at[odd, 0], zh.at[0], zs.at[0], zrs.at[0], right),
        send(base.at[odd, 1], zh.at[1], zs.at[1], zrs.at[1], left),
    )
    near_z = (
        send(base.at[near], zr.at[0], zs.at[2], zrs.at[2], right),
        send(base.at[near], zr.at[1], zs.at[3], zrs.at[3], left),
    )

    def total_y(zz):
        wait_ways(zz)
        for core in range(2):
            base[zz, core] = summed(zz, core).astype(BF16)

    def near_on():
        @pl.when(from_left)
        def _():
            far_z[1].wait_recv()
            base[near, 1] = (base[near, 1].astype(F32) + zh[1].astype(F32)).astype(BF16)
            near_z[1].start()

        @pl.when(jnp.logical_not(from_left))
        def _():
            far_z[0].wait_recv()
            base[near, 0] = (base[near, 0].astype(F32) + zh[0].astype(F32)).astype(BF16)
            near_z[0].start()

    total_y(zza)

    @pl.when(jnp.logical_not(owns))
    def _():
        start(far_z)

    rows_t = xin

    @pl.when(s == 0)
    def _():
        rows_t[...] = gt[...]
        gates_ref[0] = gate_out[0:1]

    @pl.when(s == 1)
    def _():
        rows_back.wait_recv()
        gates_back.wait_recv()
        for i in range(2):
            packed = jnp.dot(xin[i], picks, preferred_element_type=F32)
            rows_t[i] = jnp.where(live, packed + pacc[i], 0.0).astype(BF16)
        gates_ref[0] = jnp.dot(gate_in[...], picks, preferred_element_type=F32).astype(BF16)[0:1]

    rows_ref[0, 0] = (
        contract(rows_t[0], fold[0], 0, 0) + contract(rows_t[1], fold[1], 0, 0)
    ).astype(BF16)

    total_y(zzb)
    near_on()

    total = q[x * 2 + c].astype(F32)
    for step in range(1, 4):
        xx = turn(x, step)
        send(qb.at[xx], qb.at[xx], os_.at[0], or_.at[xx], east).wait_recv()
        total = total + qb[xx].astype(F32)
    cgrad_ref[0, 0] = total.astype(BF16)

    def homeward(core):
        return send(final.at[core], wg, ps.at[core], pr.at[0], device(x, z, y, core))

    @pl.when(owns)
    def _():
        near_z[0].wait_recv()
        near_z[1].wait_recv()
        for core in range(2):
            final[core] = (
                base[odd, core].astype(F32) + zr[0, core].astype(F32) + zr[1, core].astype(F32)
            ).astype(BF16)
            here = jnp.logical_and(diagonal, c == core)

            @pl.when(here)
            def _():
                wg[...] = final[core]

            @pl.when(jnp.logical_not(here))
            def _():
                homeward(core).start()

    @pl.when(jnp.logical_not(stays))
    def _():
        send(stage, wg, ps.at[0], pr.at[0], holder).wait_recv()

    wgrad_ref[0] = wg[pl.ds(0, SLAB)]

    @pl.when(owns)
    def _():
        for core in range(2):
            @pl.when(jnp.logical_not(jnp.logical_and(diagonal, c == core)))
            def _():
                homeward(core).wait_send()
        for copy in along_z():
            copy.wait_send()

    @pl.when(jnp.logical_not(owns))
    def _():
        for copy in far_z:
            copy.wait_send()

    @pl.when(from_left)
    def _():
        onward[0].wait_send()
        near_z[1].wait_send()

    @pl.when(jnp.logical_not(from_left))
    def _():
        onward[1].wait_send()
        near_z[0].wait_send()

    for copy in always:
        copy.wait_send()
    for zz, u in ((zz1, 0), (zz2, 1)):
        for copy in along_y(zz, u) + beyond_y(zz, u) + halves(zz) + ways(zz):
            copy.wait_send()

    @pl.when(jnp.logical_not(stays))
    def _():
        to_holder.wait_send()

    for step in range(4):
        to_sibling(turn(x, step)).wait_send()
        if step:
            to_column(turn(x, step)).wait_send()

    @pl.when(s == 0)
    def _():
        rows_back.wait_send()
        gates_back.wait_send()

    @pl.when(s == 1)
    def _():
        rows_in.wait_send()


def call(*operands):
    dma = pltpu.SemaphoreType.DMA
    vmem = pl.BlockSpec(memory_space=pltpu.VMEM)

    def block(*lead, kind=BF16):
        return pltpu.VMEM((*lead, PAD, LEN), kind)

    return pl.pallas_call(
        kernel,
        name="relay",
        out_shape=(
            jax.ShapeDtypeStruct((1, 1, LEN, COLS), BF16),
            jax.ShapeDtypeStruct((1, 1, LEN), BF16),
            jax.ShapeDtypeStruct((1, 1, LEN, INNER_DEV), BF16),
            jax.ShapeDtypeStruct((1, SLAB, INNER_DEV), BF16),
        ),
        in_specs=[vmem] * 4 + [pl.BlockSpec(memory_space=pltpu.SMEM), vmem],
        out_specs=(vmem,) * 4,
        scratch_shapes=[
            block(),
            block(16),
            pltpu.VMEM((8, LEN, INNER_DEV), BF16),
            block(2),
            pltpu.VMEM((2, PAD, 1), F32),
            block(2, kind=F32),
            block(2),
            block(2),
            block(2),
            pltpu.VMEM((8, LEN), F32),
            pltpu.VMEM((8, 8, LEN), F32),
            pltpu.VMEM((16, LEN), BF16),
            pltpu.VMEM((16, LEN), BF16),
            block(2),
            block(16),
            block(2, 2),
            block(2, 2, 2),
            block(2),
            block(2, 2),
            block(2, 2),
            block(2),
            block(),
            pltpu.VMEM((8, LEN, INNER_DEV), BF16),
            pltpu.VMEM((4, LEN, INNER_DEV), BF16),
            pltpu.VMEM((4, LEN, INNER_DEV), BF16),
            dma((12,)), dma((16,)), dma((3,)), dma((1,)), dma((8,)), dma((8, 2)), dma((4,)),
            dma((7,)), dma((7,)), dma((2, 2)), dma((2, 2)), dma((2, 2)), dma((2, 2)),
            dma((4,)), dma((4,)), dma((4,)), dma((4,)), dma((4,)), dma((4,)),
            pltpu.SemaphoreType.REGULAR,
        ],
        compiler_params=pltpu.CompilerParams(
            collective_id=0, has_side_effects=True, vmem_limit_bytes=56 * 2**20
        ),
    )(*operands)


def per_device(byte_rows, context, weight, keep_list, counts, gate_vector):
    return call(byte_rows, context, weight, keep_list, counts, gate_vector.reshape(1, COLS))


def solution(mesh):
    placed = (
        P("section", "dp", None, "tensor"),
        P("section", "dp", None, "tensor"),
        P("section", "dp", "tensor"),
        P("dp", None),
        P("dp"),
        P("tensor"),
    )
    return jax.shard_map(
        per_device,
        mesh=mesh,
        in_specs=placed,
        out_specs=(
            P("section", "dp", None, "tensor"),
            P("section", "dp", None),
            P("section", "dp", None, "tensor"),
            P("section", "dp", "tensor"),
        ),
        check_vma=False,
    )
```

```python
import jax
import jax.numpy as jnp
from jax import lax
from jax.experimental import pallas as pl
from jax.experimental.pallas import tpu as pltpu
from jax.sharding import PartitionSpec as P

D = 4672
SLAB = 292
PAD = 304
START, SIZE = (0, 128, 240), (128, 112, 64)
COLS = 2 * SLAB
LEN = 512
INNER_DEV = 512
EPSILON = 1e-06
SHARPNESS = 30.0

MESH = pl.DeviceIdType.MESH
F32 = jnp.float32
BF16 = jnp.bfloat16


def turn(i, step):
    return lax.rem(i + step, 4)


def send(src, dst, send_sem, recv_sem, to):
    return pltpu.make_async_remote_copy(
        src_ref=src,
        dst_ref=dst,
        send_sem=send_sem,
        recv_sem=recv_sem,
        device_id=to,
        device_id_type=MESH,
    )


def contract(a, b, axis_a, axis_b):
    return lax.dot_general(
        a, b, (((axis_a,), (axis_b,)), ((), ())), preferred_element_type=F32
    )


def kernel(
    byte_ref, ctx_ref, w_ref, keep_ref, counts_ref, g_ref,
    rows_ref, gates_ref, cgrad_ref, wgrad_ref,
    stage, wf, cf, bt, gcol, pacc, spread, e_ref, gt, st_out, st_in, gate_out, gate_in, xin,
    wp, yh, yr, zh, zr, zhb, zrb, base, final, wg, q, qa, qb,
    ws, wr, ps, pr, cs_, cr, xs, ss, sr, hs, hr, fs, fr, zs, zrs, qs, qr, os_, or_, bs, vs, vr, ready,
):
    s = lax.axis_index("section")
    d = lax.axis_index("dp")
    t = lax.axis_index("tensor")
    y, z, x, c = lax.div(d, 4), lax.rem(d, 4), lax.div(t, 2), lax.rem(t, 2)

    def device(yy, zz, xx, cc):
        return (s, yy * 4 + zz, xx * 2 + cc)

    up, down = device(turn(y, 1), z, x, c), device(turn(y, 3), z, x, c)
    right, left = device(y, turn(z, 1), x, c), device(y, turn(z, 3), x, c)
    east, west = device(y, z, turn(x, 1), c), device(y, z, turn(x, 3), c)
    sibling = device(y, z, x, 1 - c)
    partner = (1 - s, d, t)
    team = [(s, d, lax.rem(t + j, 8)) for j in range(1, 8)]
    holder = device(x, z, y, lax.div(z, 2))
    owns = lax.div(z, 2) == c
    diagonal = x == y
    stays = jnp.logical_and(diagonal, owns)

    barrier = pltpu.get_barrier_semaphore()
    hello = [up, down, right, left, partner] + team
    for peer in hello:
        pl.semaphore_signal(barrier, inc=1, device_id=peer, device_id_type=MESH)

    @pl.when(jnp.logical_not(stays))
    def _():
        pl.semaphore_signal(barrier, inc=1, device_id=holder, device_id_type=MESH)

    for core in range(2):
        @pl.when(jnp.logical_and(owns, jnp.logical_not(jnp.logical_and(diagonal, c == core))))
        def _():
            pl.semaphore_signal(
                barrier, inc=1, device_id=device(x, z, y, core), device_id_type=MESH
            )

    stage[pl.ds(PAD - 16, 16)] = jnp.zeros((16, INNER_DEV), BF16)
    stage[pl.ds(0, SLAB)] = w_ref[0]
    cf[t] = ctx_ref[0, 0]
    fold = []
    for i in range(2):
        row = lax.broadcasted_iota(jnp.int32, (PAD, COLS), 0)
        col = lax.broadcasted_iota(jnp.int32, (PAD, COLS), 1)
        hit = jnp.logical_and(col == row + i * SLAB, row < SLAB)
        fold.append(jnp.where(hit, 1.0, 0.0).astype(BF16))
    for i in range(2):
        bt[i] = jnp.dot(fold[i], byte_ref[...], preferred_element_type=F32).astype(BF16)

    greeted = (
        len(hello)
        + jnp.where(stays, 0, 1)
        + jnp.where(owns, jnp.where(diagonal, 1, 2), 0)
    )
    pl.semaphore_wait(barrier, greeted)

    def unit(yy, zz):
        return yy * 4 + zz * 2

    def pair(ref, n, h):
        return ref.at[pl.ds(n, 2), pl.ds(START[h], SIZE[h])]

    def one(ref, n, h):
        return ref.at[n, pl.ds(START[h], SIZE[h])]

    always = []

    def go(copy):
        copy.start()
        always.append(copy)

    def start(copies):
        for copy in copies:
            copy.start()

    home = x * 4 + lax.rem(z, 2) * 2 + c

    def to_holder(h):
        rows = stage.at[pl.ds(START[h], SIZE[h])]
        return send(rows, one(wf, home, h), ps.at[2, h], wr.at[home, h], holder)

    @pl.when(stays)
    def _():
        wf[home] = stage[...]

    @pl.when(jnp.logical_not(stays))
    def _():
        to_holder(0).start()

    rows_in = send(bt, xin, xs.at[0], xs.at[1], partner)
    rows_back = send(e_ref, xin, xs.at[0], xs.at[1], partner)
    gates_back = send(gate_out, gate_in, xs.at[2], xs.at[3], partner)

    @pl.when(s == 1)
    def _():
        rows_in.start()

    odd = lax.rem(z, 2)
    zz1 = jnp.where(owns, odd, 1 - odd)
    zz2 = 1 - zz1
    near = 1 - odd
    from_left = owns == (odd == 1)
    half = LEN // 2

    def context_out():
        for i, to in enumerate((east, west, sibling)):
            go(send(ctx_ref.at[0, 0], cf.at[t], cs_.at[i], cr.at[t, 0], to))

    def wait_context(it, part):
        rows = cf.at[it]
        if part is not None:
            rows = cf.at[it, pl.ds(part * half, half)]
        send(rows, rows, cs_.at[0], cr.at[it, part or 0], east).wait_recv()

    def context_on():
        for i, (xx, to) in enumerate(((turn(x, 3), east), (turn(x, 1), west))):
            it = xx * 2 + c
            wait_context(it, None)
            rows = cf.at[it, pl.ds(i * half, half)]
            go(send(rows, rows, cs_.at[3 + i], cr.at[it, i], to))
            go(send(cf.at[it], cf.at[it], cs_.at[5 + i], cr.at[it, 0], sibling))

    def context_last():
        it = turn(x, 2) * 2 + c
        wait_context(it, 0)
        wait_context(it, 1)
        go(send(cf.at[it], cf.at[it], cs_.at[7], cr.at[it, 0], sibling))
        for xx in range(4):
            wait_context(xx * 2 + 1 - c, None)

    def arrived(n, h):
        send(pair(wf, n, h), pair(wf, n, h), ws.at[0, h], wr.at[n, h], up).wait_recv()

    def arrived_block(n, h):
        send(one(wf, n, h), one(wf, n, h), ws.at[0, h], wr.at[n, h], up).wait_recv()

    def pass_pair(n, h, i, to):
        return send(pair(wf, n, h), pair(wf, n, h), ws.at[i, h], wr.at[n, h], to)

    def pass_one(n, h, i, to):
        return send(one(wf, n, h), one(wf, n, h), ws.at[i, h], wr.at[n, h], to)

    def along_y(zz, u, h):
        n = unit(y, zz)
        return pass_pair(n, h, 4 + 4 * u, up), pass_pair(n, h, 5 + 4 * u, down)

    def beyond_y(zz, u, h):
        n, m = unit(turn(y, 3), zz), unit(turn(y, 1), zz) + 1
        return pass_one(n, h, 6 + 4 * u, up), pass_one(m, h, 7 + 4 * u, down)

    def on_along_y(zz, u, h):
        ahead, back = beyond_y(zz, u, h)
        arrived(unit(turn(y, 3), zz), h)
        ahead.start()
        arrived(unit(turn(y, 1), zz), h)
        back.start()

    def along_z(h):
        n = unit(y, odd)
        return pass_pair(n, h, 1, right), pass_pair(n, h, 2, left)

    def arrived_far(yy, zz, h):
        n = unit(yy, zz)
        arrived_block(n, h)
        arrived_block(n + 1, h)

    def onward(h):
        n = unit(y, near)
        return pass_one(n, h, 3, right), pass_one(n + 1, h, 3, left)

    def on_along_z(h):
        arrived(unit(y, near), h)

        @pl.when(from_left)
        def _():
            onward(h)[0].start()

        @pl.when(jnp.logical_not(from_left))
        def _():
            onward(h)[1].start()

    def last_z(step):
        n = unit(turn(y, step), odd)
        return (
            send(pair(wf, n, 2), pair(wf, n, 2), bs.at[0, step], wr.at[n, 2], right),
            send(pair(wf, n, 2), pair(wf, n, 2), bs.at[1, step], wr.at[n, 2], left),
        )

    def last_onward(step):
        n = unit(turn(y, step), near)
        m = n + 1
        return (
            send(one(wf, n, 2), one(wf, n, 2), bs.at[2, step], wr.at[n, 2], right),
            send(one(wf, m, 2), one(wf, m, 2), bs.at[2, step], wr.at[m, 2], left),
        )

    def last_on_along_z(step):
        arrived(unit(turn(y, step), near), 2)

        @pl.when(from_left)
        def _():
            last_onward(step)[0].start()

        @pl.when(jnp.logical_not(from_left))
        def _():
            last_onward(step)[1].start()

    def project(yy, zz):
        n = unit(yy, zz)
        pacc[zz] += contract(wf[n], cf[yy * 2], 1, 1) + contract(wf[n + 1], cf[yy * 2 + 1], 1, 1)

    pacc[...] = jnp.zeros_like(pacc)

    @pl.when(jnp.logical_not(stays))
    def _():
        for h in range(2):
            to_holder(h).wait_send()
            to_holder(h + 1).start()

    @pl.when(owns)
    def _():
        for h in range(3):
            for core in range(2):
                @pl.when(jnp.logical_not(jnp.logical_and(diagonal, c == core)))
                def _():
                    arrived_block(unit(y, zz1) + core, h)
            if h < 2:
                start(along_z(h))
            start(along_y(zz1, 0, h))
        pl.semaphore_signal(ready, inc=1, device_id=sibling, device_id_type=MESH)

    @pl.when(jnp.logical_not(owns))
    def _():
        on_along_z(0)
        start(along_y(zz1, 0, 0))
        pl.semaphore_wait(ready, 1)

    context_out()

    @pl.when(owns)
    def _():
        for h in range(2):
            on_along_y(zz1, 0, h)
            on_along_z(h)
            start(along_y(zz2, 1, h))
        start(last_z(0))
        on_along_y(zz1, 0, 2)
        start(last_z(1))
        start(last_z(3))
        arrived_far(turn(y, 2), zz1, 2)
        start(last_z(2))

    @pl.when(jnp.logical_not(owns))
    def _():
        arrived_far(y, zz2, 0)
        start(along_y(zz2, 1, 0))
        on_along_z(1)
        start(along_y(zz1, 0, 1))
        arrived_far(y, zz2, 1)
        start(along_y(zz2, 1, 1))

    last_on_along_z(0)
    context_on()

    @pl.when(owns)
    def _():
        on_along_y(zz2, 1, 0)

    @pl.when(jnp.logical_not(owns))
    def _():
        on_along_y(zz1, 0, 0)

    last_on_along_z(1)
    last_on_along_z(3)

    @pl.when(owns)
    def _():
        on_along_y(zz2, 1, 1)

    @pl.when(jnp.logical_not(owns))
    def _():
        on_along_y(zz2, 1, 0)
        on_along_y(zz1, 0, 1)

    last_on_along_z(2)
    context_last()

    @pl.when(jnp.logical_not(owns))
    def _():
        for step in (0, 1, 3):
            arrived_far(turn(y, step), odd, 2)

    pick = jnp.where(
        lax.broadcasted_iota(jnp.int32, (1, LEN), 1) < counts_ref[0], keep_ref[...], -1
    )
    live = pick >= 0
    place_of = lax.broadcasted_iota(jnp.int32, (LEN, LEN), 0)
    picks = jnp.where(pick == place_of, 1.0, 0.0).astype(BF16)

    project(y, zz1)
    project(y, zz2)

    @pl.when(jnp.logical_not(owns))
    def _():
        on_along_y(zz2, 1, 1)

    project(turn(y, 1), zz1)
    project(turn(y, 3), zz1)
    for h in range(2):
        arrived_far(turn(y, 2), zz1, h)
    project(turn(y, 1), zz2)
    project(turn(y, 3), zz2)

    @pl.when(jnp.logical_not(owns))
    def _():
        arrived_far(turn(y, 2), odd, 2)

    project(turn(y, 2), zz1)

    @pl.when(s == 0)
    def _():
        rows_in.wait_recv()
        for i in range(2):
            spread[i] = contract(xin[i], picks, 1, 1).astype(BF16)

    g = g_ref[...]
    first = g.astype(BF16)
    rest = g - first.astype(F32)
    second = rest.astype(BF16)
    third = (rest - second.astype(F32)).astype(BF16)
    for i in range(2):
        terms = [contract(fold[i], jnp.broadcast_to(v, (16, COLS)), 1, 1) for v in (first, second, third)]
        gcol[i] = (terms[0] + terms[1] + terms[2])[:, 0:1]

    arrived_far(turn(y, 2), zz2, 0)
    arrived_far(turn(y, 2), zz2, 1)
    project(turn(y, 2), zz2)

    @pl.when(s == 0)
    def _():
        st_out[...] = jnp.zeros_like(st_out)
        for i in range(2):
            e = (bt[i].astype(F32) + pacc[i]).astype(BF16)
            e_ref[i] = e
            e = e.astype(F32)
            st_out[0:1] += jnp.sum(e * e, axis=0, keepdims=True)
            st_out[1:2] += jnp.sum(e * gcol[i], axis=0, keepdims=True)
        st_in[t] = st_out[...]
        stats = [
            send(st_out, st_in.at[t], ss.at[j], sr.at[j], peer) for j, peer in enumerate(team)
        ]
        for copy in stats:
            copy.start()
        rows_back.start()
        for copy in stats:
            copy.wait()
        sums = st_in[0]
        for j in range(1, 8):
            sums = sums + st_in[j]
        inverse = lax.rsqrt(sums[0:1] / D + EPSILON)
        score = inverse * sums[1:2]
        squashed = jax.nn.sigmoid(score)
        gate = (-SHARPNESS * squashed).astype(BF16)
        gate_out[...] = jnp.broadcast_to(gate, gate_out.shape)
        gates_back.start()
        slope = -SHARPNESS * squashed * (1.0 - squashed)
        pull = score * inverse * inverse / D
        for i in range(2):
            gate_part = slope * (inverse * gcol[i] - pull * e_ref[i].astype(F32))
            gt[i] = (spread[i].astype(F32) + gate_part).astype(BF16)

    @pl.when(s == 1)
    def _():
        for i in range(2):
            rows = bt[i]
            gt[i] = jnp.where(live, rows, jnp.zeros_like(rows))

    zza = jnp.where(owns, near, odd)
    zzb = 1 - zza

    def products(yy, zz):
        n = unit(yy, zz)
        for core in range(2):
            wp[n + core] = jnp.dot(
                gt[zz], cf[yy * 2 + core], preferred_element_type=F32
            ).astype(BF16)

    def halves(zz, h):
        n = unit(turn(y, 2), zz)
        return (
            send(one(wp, n, h), yh.at[0, zz, pl.ds(START[h], SIZE[h])], hs.at[0, zz, h], hr.at[0, zz, h], up),
            send(one(wp, n + 1, h), yh.at[1, zz, pl.ds(START[h], SIZE[h])], hs.at[1, zz, h], hr.at[1, zz, h], down),
        )

    def ways(zz, h):
        n, m = unit(turn(y, 1), zz), unit(turn(y, 3), zz)
        return (
            send(pair(wp, n, h), pair(yr, zz * 2, h), fs.at[0, zz, h], fr.at[0, zz, h], up),
            send(pair(wp, m, h), pair(yr, 4 + zz * 2, h), fs.at[1, zz, h], fr.at[1, zz, h], down),
        )

    def merge(zz, h):
        rows = pl.ds(START[h], SIZE[h])
        to_up, to_down = halves(zz, h)
        on_up, on_down = ways(zz, h)
        n = unit(turn(y, 1), zz)
        to_up.wait_recv()
        wp[n, rows] = (wp[n, rows].astype(F32) + yh[0, zz, rows].astype(F32)).astype(BF16)
        on_up.start()
        n = unit(turn(y, 3), zz) + 1
        to_down.wait_recv()
        wp[n, rows] = (wp[n, rows].astype(F32) + yh[1, zz, rows].astype(F32)).astype(BF16)
        on_down.start()

    rows2 = pl.ds(START[2], SIZE[2])

    def last_far(step):
        n = unit(turn(y, step), odd)
        return (
            send(one(wp, n, 2), zhb.at[step * 2], vs.at[0, step], vr.at[0, step], right),
            send(one(wp, n + 1, 2), zhb.at[step * 2 + 1], vs.at[1, step], vr.at[1, step], left),
        )

    def last_near(step):
        n = unit(turn(y, step), near)
        return (
            send(
                pair(wp, n, 2), zrb.at[pl.ds(step * 4, 2)],
                vs.at[2, step], vr.at[2, step], right,
            ),
            send(
                pair(wp, n, 2), zrb.at[pl.ds(step * 4 + 2, 2)],
                vs.at[3, step], vr.at[3, step], left,
            ),
        )

    def last_far_out(*steps):
        @pl.when(jnp.logical_not(owns))
        def _():
            for step in steps:
                start(last_far(step))

    def last_near_on(step):
        def add(way):
            last_far(step)[way].wait_recv()
            n = unit(turn(y, step), near) + way
            wp[n, rows2] = (wp[n, rows2].astype(F32) + zhb[step * 2 + way].astype(F32)).astype(BF16)
            last_near(step)[way].start()

        @pl.when(from_left)
        def _():
            add(1)

        @pl.when(jnp.logical_not(from_left))
        def _():
            add(0)

    def last_sum(step):
        for copy in last_near(step):
            copy.wait_recv()
        for core in range(2):
            n = unit(turn(y, step), odd) + core
            total = wp[n, rows2].astype(F32)
            for way in range(2):
                total = total + zrb[step * 4 + way * 2 + core].astype(F32)
            wp[n, rows2] = total.astype(BF16)

    products(turn(y, 2), zza)
    start(halves(zza, 0))
    start(halves(zza, 1))
    last_far_out(2)
    products(turn(y, 1), zza)
    products(turn(y, 3), zza)
    last_far_out(1, 3)
    products(turn(y, 2), zzb)
    merge(zza, 0)
    start(halves(zzb, 0))
    merge(zza, 1)
    start(halves(zzb, 1))
    products(turn(y, 1), zzb)
    products(turn(y, 3), zzb)
    products(y, zza)
    last_far_out(0)
    products(y, zzb)
    last_near_on(2)
    last_near_on(1)
    last_near_on(3)
    merge(zzb, 0)
    merge(zzb, 1)
    last_near_on(0)

    @pl.when(owns)
    def _():
        last_sum(2)
        start(halves(odd, 2))

    def to_sibling(xx):
        return send(q.at[xx * 2 + 1 - c], qa.at[xx], qs.at[xx], qr.at[xx], sibling)

    def to_column(xx):
        return send(q.at[xx * 2 + c], qb.at[x], os_.at[xx], or_.at[x], device(y, z, xx, c))

    def context_part(it):
        n = lax.div(it, 2) * 4 + lax.rem(it, 2)
        return contract(gt[0], wf[n], 0, 0) + contract(gt[1], wf[n + 2], 0, 0)

    @pl.loop(0, 4)
    def _(j):
        xx = turn(x, j + 1)
        q[xx * 2 + 1 - c] = context_part(xx * 2 + 1 - c).astype(BF16)
        to_sibling(xx).start()

    @pl.loop(0, 4)
    def _(j):
        xx = turn(x, j + 1)
        part = context_part(xx * 2 + c)
        to_sibling(xx).wait_recv()
        q[xx * 2 + c] = (part + qa[xx].astype(F32)).astype(BF16)

        @pl.when(j < 3)
        def _():
            to_column(xx).start()

    def far_z(h):
        return (
            send(one(base, odd * 2, h), one(zh, 0, h), zs.at[0, h], zrs.at[0, h], right),
            send(one(base, odd * 2 + 1, h), one(zh, 1, h), zs.at[1, h], zrs.at[1, h], left),
        )

    def near_z(h):
        return (
            send(pair(base, near * 2, h), pair(zr, 0, h), zs.at[2, h], zrs.at[2, h], right),
            send(pair(base, near * 2, h), pair(zr, 2, h), zs.at[3, h], zrs.at[3, h], left),
        )

    def total_y(zz, h):
        rows = pl.ds(START[h], SIZE[h])
        for copy in ways(zz, h):
            copy.wait_recv()
        for core in range(2):
            total = wp[unit(y, zz) + core, rows].astype(F32)
            for way in range(2):
                total = total + yr[way * 4 + zz * 2 + core, rows].astype(F32)
            base[zz * 2 + core, rows] = total.astype(BF16)

    def near_on(h):
        rows = pl.ds(START[h], SIZE[h])

        def add(way):
            far_z(h)[way].wait_recv()
            n = near * 2 + way
            base[n, rows] = (base[n, rows].astype(F32) + zh[way, rows].astype(F32)).astype(BF16)
            near_z(h)[way].start()

        @pl.when(from_left)
        def _():
            add(1)

        @pl.when(jnp.logical_not(from_left))
        def _():
            add(0)

    def homeward(core, h):
        rows = wg.at[pl.ds(START[h], SIZE[h])]
        return send(one(final, core, h), rows, ps.at[core, h], pr.at[h], device(x, z, y, core))

    def finish(h):
        rows = pl.ds(START[h], SIZE[h])
        if h < 2:
            near_z(h)[0].wait_recv()
            near_z(h)[1].wait_recv()
        for core in range(2):
            total = base[odd * 2 + core, rows].astype(F32)
            for way in range(2 if h < 2 else 0):
                total = total + zr[way * 2 + core, rows].astype(F32)
            final[core, rows] = total.astype(BF16)
            here = jnp.logical_and(diagonal, c == core)

            @pl.when(here)
            def _():
                wg[rows] = final[core, rows]

            @pl.when(jnp.logical_not(here))
            def _():
                homeward(core, h).start()

    @pl.when(owns)
    def _():
        last_sum(1)
        last_sum(3)
        merge(odd, 2)
        last_sum(0)

    for h in range(2):
        total_y(zza, h)

        @pl.when(jnp.logical_not(owns))
        def _():
            start(far_z(h))

    @pl.when(owns)
    def _():
        near_on(0)
        near_on(1)

    rows_t = xin

    @pl.when(s == 0)
    def _():
        rows_t[...] = gt[...]
        gates_ref[0] = gate_out[0:1]

    @pl.when(s == 1)
    def _():
        rows_back.wait_recv()
        gates_back.wait_recv()
        for i in range(2):
            packed = jnp.dot(xin[i], picks, preferred_element_type=F32)
            rows_t[i] = jnp.where(live, packed + pacc[i], 0.0).astype(BF16)
        gates_ref[0] = jnp.dot(gate_in[...], picks, preferred_element_type=F32).astype(BF16)[0:1]

    rows_ref[...] = (
        contract(fold[0], rows_t[0], 0, 0) + contract(fold[1], rows_t[1], 0, 0)
    ).astype(BF16)

    @pl.when(owns)
    def _():
        total_y(odd, 2)
        finish(2)

    for h in range(2):
        total_y(zzb, h)

        @pl.when(owns)
        def _():
            finish(h)

        @pl.when(jnp.logical_not(owns))
        def _():
            near_on(h)

    total = q[x * 2 + c].astype(F32)
    for step in range(1, 4):
        xx = turn(x, step)
        send(qb.at[xx], qb.at[xx], os_.at[0], or_.at[xx], east).wait_recv()
        total = total + qb[xx].astype(F32)
    cgrad_ref[0, 0] = total.astype(BF16)

    @pl.when(jnp.logical_not(stays))
    def _():
        for h in range(3):
            rows = wg.at[pl.ds(START[h], SIZE[h])]
            send(rows, rows, ps.at[0, h], pr.at[h], holder).wait_recv()

    wgrad_ref[0] = wg[pl.ds(0, SLAB)]

    def left_already(copies):
        for copy in copies:
            copy.wait_send()

    @pl.when(owns)
    def _():
        for h in range(3):
            for core in range(2):
                @pl.when(jnp.logical_not(jnp.logical_and(diagonal, c == core)))
                def _():
                    homeward(core, h).wait_send()
        for h in range(2):
            left_already(along_z(h))
        left_already(along_y(zz1, 0, 2) + beyond_y(zz1, 0, 2))
        left_already(halves(odd, 2) + ways(odd, 2))
        for step in range(4):
            left_already(last_z(step))

    @pl.when(jnp.logical_not(owns))
    def _():
        for h in range(2):
            left_already(far_z(h))
        for step in range(4):
            left_already(last_far(step))

    def one_way(onward_way, near_way):
        for h in range(2):
            onward(h)[onward_way].wait_send()
            near_z(h)[near_way].wait_send()
        for step in range(4):
            last_onward(step)[onward_way].wait_send()
            last_near(step)[near_way].wait_send()

    @pl.when(from_left)
    def _():
        one_way(0, 1)

    @pl.when(jnp.logical_not(from_left))
    def _():
        one_way(1, 0)

    for h in range(2):
        for zz, u in ((zz1, 0), (zz2, 1)):
            left_already(along_y(zz, u, h) + beyond_y(zz, u, h) + halves(zz, h) + ways(zz, h))

    @pl.when(jnp.logical_not(stays))
    def _():
        to_holder(2).wait_send()

    for copy in always:
        copy.wait_send()
    for step in range(4):
        to_sibling(turn(x, step)).wait_send()
        if step:
            to_column(turn(x, step)).wait_send()

    @pl.when(s == 0)
    def _():
        rows_back.wait_send()
        gates_back.wait_send()

    @pl.when(s == 1)
    def _():
        rows_in.wait_send()


def call(*operands):
    dma = pltpu.SemaphoreType.DMA
    vmem = pl.BlockSpec(memory_space=pltpu.VMEM)

    def block(*lead, kind=BF16):
        return pltpu.VMEM((*lead, PAD, LEN), kind)

    return pl.pallas_call(
        kernel,
        name="relay",
        out_shape=(
            jax.ShapeDtypeStruct((COLS, LEN), BF16),
            jax.ShapeDtypeStruct((1, 1, LEN), BF16),
            jax.ShapeDtypeStruct((1, 1, LEN, INNER_DEV), BF16),
            jax.ShapeDtypeStruct((1, SLAB, INNER_DEV), BF16),
        ),
        in_specs=[vmem] * 4 + [pl.BlockSpec(memory_space=pltpu.SMEM), vmem],
        out_specs=(vmem,) * 4,
        scratch_shapes=[
            block(),
            block(16),
            pltpu.VMEM((8, LEN, INNER_DEV), BF16),
            block(2),
            pltpu.VMEM((2, PAD, 1), F32),
            block(2, kind=F32),
            block(2),
            block(2),
            block(2),
            pltpu.VMEM((8, LEN), F32),
            pltpu.VMEM((8, 8, LEN), F32),
            pltpu.VMEM((16, LEN), BF16),
            pltpu.VMEM((16, LEN), BF16),
            block(2),
            block(16),
            block(2, 2),
            block(8),
            block(2),
            block(4),
            pltpu.VMEM((8, SIZE[2], LEN), BF16),
            pltpu.VMEM((16, SIZE[2], LEN), BF16),
            block(4),
            block(2),
            block(),
            pltpu.VMEM((8, LEN, INNER_DEV), BF16),
            pltpu.VMEM((4, LEN, INNER_DEV), BF16),
            pltpu.VMEM((4, LEN, INNER_DEV), BF16),
            dma((12, 3)), dma((16, 3)), dma((3, 3)), dma((3,)), dma((8,)), dma((8, 2)), dma((4,)),
            dma((7,)), dma((7,)), dma((2, 2, 3)), dma((2, 2, 3)), dma((2, 2, 3)), dma((2, 2, 3)),
            dma((4, 2)), dma((4, 2)), dma((4,)), dma((4,)), dma((4,)), dma((4,)),
            dma((3, 4)), dma((4, 4)), dma((4, 4)),
            pltpu.SemaphoreType.REGULAR,
        ],
        compiler_params=pltpu.CompilerParams(
            collective_id=0, has_side_effects=True, vmem_limit_bytes=56 * 2**20
        ),
    )(*operands)


def per_device(byte_rows, context, weight, keep_list, counts, gate_vector):
    rows, gates, context_grad, weight_grad = call(
        byte_rows[0, 0].T, context, weight, keep_list, counts, gate_vector.reshape(1, COLS)
    )
    return rows.T[None, None], gates, context_grad, weight_grad


def solution(mesh):
    placed = (
        P("section", "dp", None, "tensor"),
        P("section", "dp", None, "tensor"),
        P("section", "dp", "tensor"),
        P("dp", None),
        P("dp"),
        P("tensor"),
    )
    return jax.shard_map(
        per_device,
        mesh=mesh,
        in_specs=placed,
        out_specs=(
            P("section", "dp", None, "tensor"),
            P("section", "dp", None),
            P("section", "dp", None, "tensor"),
            P("section", "dp", "tensor"),
        ),
        check_vma=False,
    )
```

```python
import jax
import jax.numpy as jnp
from jax import lax
from jax.experimental import pallas as pl
from jax.experimental.pallas import tpu as pltpu
from jax.sharding import PartitionSpec as P

D = 4672
SLAB = 292
PAD = 304
START, SIZE = (0, 128, 240), (128, 112, 64)
COLS = 2 * SLAB
LEN = 512
INNER_DEV = 512
EPSILON = 1e-06
SHARPNESS = 30.0

MESH = pl.DeviceIdType.MESH
F32 = jnp.float32
BF16 = jnp.bfloat16


def turn(i, step):
    return lax.rem(i + step, 4)


def send(src, dst, send_sem, recv_sem, to):
    return pltpu.make_async_remote_copy(
        src_ref=src,
        dst_ref=dst,
        send_sem=send_sem,
        recv_sem=recv_sem,
        device_id=to,
        device_id_type=MESH,
    )


def contract(a, b, axis_a, axis_b):
    return lax.dot_general(
        a, b, (((axis_a,), (axis_b,)), ((), ())), preferred_element_type=F32
    )


def kernel(
    byte_ref, ctx_ref, w_ref, keep_ref, counts_ref, g_ref,
    rows_ref, gates_ref, cgrad_ref, wgrad_ref,
    stage, wf, cf, bt, gcol, pacc, spread, e_ref, gt, st_out, st_in, gate_out, gate_in, xin,
    wp, yh, yr, zh, zr, zhb, zrb, base, final, wg, q, qa, qb,
    ws, wr, ps, pr, cs_, cr, xs, ss, sr, hs, hr, fs, fr, zs, zrs, qs, qr, os_, or_, bs, vs, vr, ready,
):
    s = lax.axis_index("section")
    d = lax.axis_index("dp")
    t = lax.axis_index("tensor")
    y, z, x, c = lax.div(d, 4), lax.rem(d, 4), lax.div(t, 2), lax.rem(t, 2)

    def device(yy, zz, xx, cc):
        return (s, yy * 4 + zz, xx * 2 + cc)

    up, down = device(turn(y, 1), z, x, c), device(turn(y, 3), z, x, c)
    right, left = device(y, turn(z, 1), x, c), device(y, turn(z, 3), x, c)
    east, west = device(y, z, turn(x, 1), c), device(y, z, turn(x, 3), c)
    sibling = device(y, z, x, 1 - c)
    partner = (1 - s, d, t)
    team = [(s, d, lax.rem(t + j, 8)) for j in range(1, 8)]
    holder = device(x, z, y, lax.div(z, 2))
    owns = lax.div(z, 2) == c
    diagonal = x == y
    stays = jnp.logical_and(diagonal, owns)

    barrier = pltpu.get_barrier_semaphore()
    hello = [up, down, right, left, partner] + team
    for peer in hello:
        pl.semaphore_signal(barrier, inc=1, device_id=peer, device_id_type=MESH)

    @pl.when(jnp.logical_not(stays))
    def _():
        pl.semaphore_signal(barrier, inc=1, device_id=holder, device_id_type=MESH)

    for core in range(2):
        @pl.when(jnp.logical_and(owns, jnp.logical_not(jnp.logical_and(diagonal, c == core))))
        def _():
            pl.semaphore_signal(
                barrier, inc=1, device_id=device(x, z, y, core), device_id_type=MESH
            )

    stage[pl.ds(PAD - 16, 16)] = jnp.zeros((16, INNER_DEV), BF16)
    stage[pl.ds(0, SLAB)] = w_ref[0]
    cf[t] = ctx_ref[0, 0]
    fold = []
    for i in range(2):
        row = lax.broadcasted_iota(jnp.int32, (PAD, COLS), 0)
        col = lax.broadcasted_iota(jnp.int32, (PAD, COLS), 1)
        hit = jnp.logical_and(col == row + i * SLAB, row < SLAB)
        fold.append(jnp.where(hit, 1.0, 0.0).astype(BF16))
    for i in range(2):
        bt[i] = jnp.dot(fold[i], byte_ref[...], preferred_element_type=F32).astype(BF16)

    greeted = (
        len(hello)
        + jnp.where(stays, 0, 1)
        + jnp.where(owns, jnp.where(diagonal, 1, 2), 0)
    )
    pl.semaphore_wait(barrier, greeted)

    def unit(yy, zz):
        return yy * 4 + zz * 2

    def pair(ref, n, h):
        return ref.at[pl.ds(n, 2), pl.ds(START[h], SIZE[h])]

    def one(ref, n, h):
        return ref.at[n, pl.ds(START[h], SIZE[h])]

    always = []

    def go(copy):
        copy.start()
        always.append(copy)

    def start(copies):
        for copy in copies:
            copy.start()

    home = x * 4 + lax.rem(z, 2) * 2 + c

    def to_holder(h):
        rows = stage.at[pl.ds(START[h], SIZE[h])]
        return send(rows, one(wf, home, h), ps.at[2, h], wr.at[home, h], holder)

    @pl.when(stays)
    def _():
        wf[home] = stage[...]

    @pl.when(jnp.logical_not(stays))
    def _():
        to_holder(0).start()

    rows_in = send(bt, xin, xs.at[0], xs.at[1], partner)
    rows_back = send(e_ref, xin, xs.at[0], xs.at[1], partner)
    gates_back = send(gate_out, gate_in, xs.at[2], xs.at[3], partner)

    @pl.when(s == 1)
    def _():
        rows_in.start()

    odd = lax.rem(z, 2)
    zz1 = jnp.where(owns, odd, 1 - odd)
    zz2 = 1 - zz1
    near = 1 - odd
    from_left = owns == (odd == 1)
    half = LEN // 2

    def context_out():
        for i, to in enumerate((east, west, sibling)):
            go(send(ctx_ref.at[0, 0], cf.at[t], cs_.at[i], cr.at[t, 0], to))

    def wait_context(it, part):
        rows = cf.at[it]
        if part is not None:
            rows = cf.at[it, pl.ds(part * half, half)]
        send(rows, rows, cs_.at[0], cr.at[it, part or 0], east).wait_recv()

    def context_on():
        for i, (xx, to) in enumerate(((turn(x, 3), east), (turn(x, 1), west))):
            it = xx * 2 + c
            wait_context(it, None)
            rows = cf.at[it, pl.ds(i * half, half)]
            go(send(rows, rows, cs_.at[3 + i], cr.at[it, i], to))
            go(send(cf.at[it], cf.at[it], cs_.at[5 + i], cr.at[it, 0], sibling))

    def context_last():
        it = turn(x, 2) * 2 + c
        wait_context(it, 0)
        wait_context(it, 1)
        go(send(cf.at[it], cf.at[it], cs_.at[7], cr.at[it, 0], sibling))
        for xx in range(4):
            wait_context(xx * 2 + 1 - c, None)

    def arrived(n, h):
        send(pair(wf, n, h), pair(wf, n, h), ws.at[0, h], wr.at[n, h], up).wait_recv()

    def arrived_block(n, h):
        send(one(wf, n, h), one(wf, n, h), ws.at[0, h], wr.at[n, h], up).wait_recv()

    def pass_pair(n, h, i, to):
        return send(pair(wf, n, h), pair(wf, n, h), ws.at[i, h], wr.at[n, h], to)

    def pass_one(n, h, i, to):
        return send(one(wf, n, h), one(wf, n, h), ws.at[i, h], wr.at[n, h], to)

    def along_y(zz, u, h):
        n = unit(y, zz)
        return pass_pair(n, h, 4 + 4 * u, up), pass_pair(n, h, 5 + 4 * u, down)

    def beyond_y(zz, u, h):
        n, m = unit(turn(y, 3), zz), unit(turn(y, 1), zz) + 1
        return pass_one(n, h, 6 + 4 * u, up), pass_one(m, h, 7 + 4 * u, down)

    def on_along_y(zz, u, h):
        ahead, back = beyond_y(zz, u, h)
        arrived(unit(turn(y, 3), zz), h)
        ahead.start()
        arrived(unit(turn(y, 1), zz), h)
        back.start()

    def along_z(h):
        n = unit(y, odd)
        return pass_pair(n, h, 1, right), pass_pair(n, h, 2, left)

    def arrived_far(yy, zz, h):
        n = unit(yy, zz)
        arrived_block(n, h)
        arrived_block(n + 1, h)

    def onward(h):
        n = unit(y, near)
        return pass_one(n, h, 3, right), pass_one(n + 1, h, 3, left)

    def on_along_z(h):
        arrived(unit(y, near), h)

        @pl.when(from_left)
        def _():
            onward(h)[0].start()

        @pl.when(jnp.logical_not(from_left))
        def _():
            onward(h)[1].start()

    def last_z(step):
        n = unit(turn(y, step), odd)
        return (
            send(pair(wf, n, 2), pair(wf, n, 2), bs.at[0, step], wr.at[n, 2], right),
            send(pair(wf, n, 2), pair(wf, n, 2), bs.at[1, step], wr.at[n, 2], left),
        )

    def last_onward(step):
        n = unit(turn(y, step), near)
        m = n + 1
        return (
            send(one(wf, n, 2), one(wf, n, 2), bs.at[2, step], wr.at[n, 2], right),
            send(one(wf, m, 2), one(wf, m, 2), bs.at[2, step], wr.at[m, 2], left),
        )

    def last_on_along_z(step):
        arrived(unit(turn(y, step), near), 2)

        @pl.when(from_left)
        def _():
            last_onward(step)[0].start()

        @pl.when(jnp.logical_not(from_left))
        def _():
            last_onward(step)[1].start()

    def project(yy, zz):
        n = unit(yy, zz)
        pacc[zz] += contract(wf[n], cf[yy * 2], 1, 1) + contract(wf[n + 1], cf[yy * 2 + 1], 1, 1)

    pacc[...] = jnp.zeros_like(pacc)

    @pl.when(jnp.logical_not(stays))
    def _():
        for h in range(2):
            to_holder(h).wait_send()
            to_holder(h + 1).start()

    @pl.when(owns)
    def _():
        for h in range(3):
            for core in range(2):
                @pl.when(jnp.logical_not(jnp.logical_and(diagonal, c == core)))
                def _():
                    arrived_block(unit(y, zz1) + core, h)
            if h < 2:
                start(along_z(h))
            start(along_y(zz1, 0, h))
        pl.semaphore_signal(ready, inc=1, device_id=sibling, device_id_type=MESH)

    @pl.when(jnp.logical_not(owns))
    def _():
        on_along_z(0)
        start(along_y(zz1, 0, 0))
        pl.semaphore_wait(ready, 1)

    context_out()

    @pl.when(owns)
    def _():
        for h in range(2):
            on_along_y(zz1, 0, h)
            on_along_z(h)
            start(along_y(zz2, 1, h))
        start(last_z(0))
        on_along_y(zz1, 0, 2)
        start(last_z(1))
        start(last_z(3))
        arrived_far(turn(y, 2), zz1, 2)
        start(last_z(2))

    @pl.when(jnp.logical_not(owns))
    def _():
        arrived_far(y, zz2, 0)
        start(along_y(zz2, 1, 0))
        on_along_z(1)
        start(along_y(zz1, 0, 1))
        arrived_far(y, zz2, 1)
        start(along_y(zz2, 1, 1))

    last_on_along_z(0)
    context_on()

    @pl.when(owns)
    def _():
        on_along_y(zz2, 1, 0)

    @pl.when(jnp.logical_not(owns))
    def _():
        on_along_y(zz1, 0, 0)

    last_on_along_z(1)
    last_on_along_z(3)

    @pl.when(owns)
    def _():
        on_along_y(zz2, 1, 1)

    @pl.when(jnp.logical_not(owns))
    def _():
        on_along_y(zz2, 1, 0)
        on_along_y(zz1, 0, 1)

    last_on_along_z(2)
    context_last()

    @pl.when(jnp.logical_not(owns))
    def _():
        for step in (0, 1, 3):
            arrived_far(turn(y, step), odd, 2)

    pick = jnp.where(
        lax.broadcasted_iota(jnp.int32, (1, LEN), 1) < counts_ref[0], keep_ref[...], -1
    )
    live = pick >= 0
    place_of = lax.broadcasted_iota(jnp.int32, (LEN, LEN), 0)
    picks = jnp.where(pick == place_of, 1.0, 0.0).astype(BF16)

    project(y, zz1)
    project(y, zz2)

    @pl.when(jnp.logical_not(owns))
    def _():
        on_along_y(zz2, 1, 1)

    project(turn(y, 1), zz1)
    project(turn(y, 3), zz1)
    for h in range(2):
        arrived_far(turn(y, 2), zz1, h)
    project(turn(y, 1), zz2)
    project(turn(y, 3), zz2)

    @pl.when(jnp.logical_not(owns))
    def _():
        arrived_far(turn(y, 2), odd, 2)

    project(turn(y, 2), zz1)

    g = g_ref[...].reshape(1, COLS)
    first = g.astype(BF16)
    rest = g - first.astype(F32)
    second = rest.astype(BF16)
    third = (rest - second.astype(F32)).astype(BF16)
    for i in range(2):
        terms = [contract(fold[i], jnp.broadcast_to(v, (16, COLS)), 1, 1) for v in (first, second, third)]
        gcol[i] = (terms[0] + terms[1] + terms[2])[:, 0:1]

    arrived_far(turn(y, 2), zz2, 0)
    arrived_far(turn(y, 2), zz2, 1)
    project(turn(y, 2), zz2)

    @pl.when(s == 0)
    def _():
        st_out[...] = jnp.zeros_like(st_out)
        for i in range(2):
            e = (bt[i].astype(F32) + pacc[i]).astype(BF16)
            e_ref[i] = e
            e = e.astype(F32)
            st_out[0:1] += jnp.sum(e * e, axis=0, keepdims=True)
            st_out[1:2] += jnp.sum(e * gcol[i], axis=0, keepdims=True)
        st_in[t] = st_out[...]
        stats = [
            send(st_out, st_in.at[t], ss.at[j], sr.at[j], peer) for j, peer in enumerate(team)
        ]
        for copy in stats:
            copy.start()
        rows_back.start()
        rows_in.wait_recv()
        for i in range(2):
            spread[i] = contract(xin[i], picks, 1, 1).astype(BF16)
        for copy in stats:
            copy.wait()
        sums = st_in[0]
        for j in range(1, 8):
            sums = sums + st_in[j]
        inverse = lax.rsqrt(sums[0:1] / D + EPSILON)
        score = inverse * sums[1:2]
        squashed = jax.nn.sigmoid(score)
        gate = (-SHARPNESS * squashed).astype(BF16)
        gate_out[...] = jnp.broadcast_to(gate, gate_out.shape)
        gates_back.start()
        slope = -SHARPNESS * squashed * (1.0 - squashed)
        pull = score * inverse * inverse / D
        for i in range(2):
            gate_part = slope * (inverse * gcol[i] - pull * e_ref[i].astype(F32))
            gt[i] = (spread[i].astype(F32) + gate_part).astype(BF16)

    @pl.when(s == 1)
    def _():
        for i in range(2):
            rows = bt[i]
            gt[i] = jnp.where(live, rows, jnp.zeros_like(rows))

    zza = jnp.where(owns, near, odd)
    zzb = 1 - zza

    def products(yy, zz):
        n = unit(yy, zz)
        for core in range(2):
            wp[n + core] = jnp.dot(
                gt[zz], cf[yy * 2 + core], preferred_element_type=F32
            ).astype(BF16)

    def halves(zz, h):
        n = unit(turn(y, 2), zz)
        return (
            send(one(wp, n, h), yh.at[0, zz, pl.ds(START[h], SIZE[h])], hs.at[0, zz, h], hr.at[0, zz, h], up),
            send(one(wp, n + 1, h), yh.at[1, zz, pl.ds(START[h], SIZE[h])], hs.at[1, zz, h], hr.at[1, zz, h], down),
        )

    def ways(zz, h):
        n, m = unit(turn(y, 1), zz), unit(turn(y, 3), zz)
        return (
            send(pair(wp, n, h), pair(yr, zz * 2, h), fs.at[0, zz, h], fr.at[0, zz, h], up),
            send(pair(wp, m, h), pair(yr, 4 + zz * 2, h), fs.at[1, zz, h], fr.at[1, zz, h], down),
        )

    def merge(zz, h):
        rows = pl.ds(START[h], SIZE[h])
        to_up, to_down = halves(zz, h)
        on_up, on_down = ways(zz, h)
        n = unit(turn(y, 1), zz)
        to_up.wait_recv()
        wp[n, rows] = (wp[n, rows].astype(F32) + yh[0, zz, rows].astype(F32)).astype(BF16)
        on_up.start()
        n = unit(turn(y, 3), zz) + 1
        to_down.wait_recv()
        wp[n, rows] = (wp[n, rows].astype(F32) + yh[1, zz, rows].astype(F32)).astype(BF16)
        on_down.start()

    rows2 = pl.ds(START[2], SIZE[2])

    def last_far(step):
        n = unit(turn(y, step), odd)
        return (
            send(one(wp, n, 2), zhb.at[step * 2], vs.at[0, step], vr.at[0, step], right),
            send(one(wp, n + 1, 2), zhb.at[step * 2 + 1], vs.at[1, step], vr.at[1, step], left),
        )

    def last_near(step):
        n = unit(turn(y, step), near)
        return (
            send(
                pair(wp, n, 2), zrb.at[pl.ds(step * 4, 2)],
                vs.at[2, step], vr.at[2, step], right,
            ),
            send(
                pair(wp, n, 2), zrb.at[pl.ds(step * 4 + 2, 2)],
                vs.at[3, step], vr.at[3, step], left,
            ),
        )

    def last_far_out(*steps):
        @pl.when(jnp.logical_not(owns))
        def _():
            for step in steps:
                start(last_far(step))

    def last_near_on(step):
        def add(way):
            last_far(step)[way].wait_recv()
            n = unit(turn(y, step), near) + way
            wp[n, rows2] = (wp[n, rows2].astype(F32) + zhb[step * 2 + way].astype(F32)).astype(BF16)
            last_near(step)[way].start()

        @pl.when(from_left)
        def _():
            add(1)

        @pl.when(jnp.logical_not(from_left))
        def _():
            add(0)

    def last_sum(step):
        for copy in last_near(step):
            copy.wait_recv()
        for core in range(2):
            n = unit(turn(y, step), odd) + core
            total = wp[n, rows2].astype(F32)
            for way in range(2):
                total = total + zrb[step * 4 + way * 2 + core].astype(F32)
            wp[n, rows2] = total.astype(BF16)

    products(turn(y, 2), zza)
    start(halves(zza, 0))
    last_far_out(2)
    products(turn(y, 2), zzb)
    start(halves(zzb, 0))
    products(turn(y, 1), zza)
    products(turn(y, 3), zza)
    last_far_out(1, 3)
    merge(zza, 0)
    start(halves(zza, 1))
    start(halves(zzb, 1))
    products(turn(y, 1), zzb)
    products(turn(y, 3), zzb)
    merge(zzb, 0)
    products(y, zza)
    last_far_out(0)
    products(y, zzb)
    last_near_on(2)
    last_near_on(1)
    merge(zza, 1)
    last_near_on(3)
    merge(zzb, 1)
    last_near_on(0)

    @pl.when(owns)
    def _():
        last_sum(2)
        start(halves(odd, 2))

    def to_sibling(xx):
        return send(q.at[xx * 2 + 1 - c], qa.at[xx], qs.at[xx], qr.at[xx], sibling)

    def to_column(xx):
        return send(q.at[xx * 2 + c], qb.at[x], os_.at[xx], or_.at[x], device(y, z, xx, c))

    def context_part(it):
        n = lax.div(it, 2) * 4 + lax.rem(it, 2)
        return contract(gt[0], wf[n], 0, 0) + contract(gt[1], wf[n + 2], 0, 0)

    @pl.loop(0, 4)
    def _(j):
        xx = turn(x, j + 1)
        q[xx * 2 + 1 - c] = context_part(xx * 2 + 1 - c).astype(BF16)
        to_sibling(xx).start()

    @pl.loop(0, 4)
    def _(j):
        xx = turn(x, j + 1)
        part = context_part(xx * 2 + c)
        to_sibling(xx).wait_recv()
        q[xx * 2 + c] = (part + qa[xx].astype(F32)).astype(BF16)

        @pl.when(j < 3)
        def _():
            to_column(xx).start()

    def far_z(h):
        return (
            send(one(base, odd * 2, h), one(zh, 0, h), zs.at[0, h], zrs.at[0, h], right),
            send(one(base, odd * 2 + 1, h), one(zh, 1, h), zs.at[1, h], zrs.at[1, h], left),
        )

    def near_z(h):
        return (
            send(pair(base, near * 2, h), pair(zr, 0, h), zs.at[2, h], zrs.at[2, h], right),
            send(pair(base, near * 2, h), pair(zr, 2, h), zs.at[3, h], zrs.at[3, h], left),
        )

    def total_y(zz, h):
        rows = pl.ds(START[h], SIZE[h])
        for copy in ways(zz, h):
            copy.wait_recv()
        for core in range(2):
            total = wp[unit(y, zz) + core, rows].astype(F32)
            for way in range(2):
                total = total + yr[way * 4 + zz * 2 + core, rows].astype(F32)
            base[zz * 2 + core, rows] = total.astype(BF16)

    def near_on(h):
        rows = pl.ds(START[h], SIZE[h])

        def add(way):
            far_z(h)[way].wait_recv()
            n = near * 2 + way
            base[n, rows] = (base[n, rows].astype(F32) + zh[way, rows].astype(F32)).astype(BF16)
            near_z(h)[way].start()

        @pl.when(from_left)
        def _():
            add(1)

        @pl.when(jnp.logical_not(from_left))
        def _():
            add(0)

    def homeward(core, h):
        rows = wg.at[pl.ds(START[h], SIZE[h])]
        return send(one(final, core, h), rows, ps.at[core, h], pr.at[h], device(x, z, y, core))

    def finish(h):
        rows = pl.ds(START[h], SIZE[h])
        if h < 2:
            near_z(h)[0].wait_recv()
            near_z(h)[1].wait_recv()
        for core in range(2):
            total = base[odd * 2 + core, rows].astype(F32)
            for way in range(2 if h < 2 else 0):
                total = total + zr[way * 2 + core, rows].astype(F32)
            final[core, rows] = total.astype(BF16)
            here = jnp.logical_and(diagonal, c == core)

            @pl.when(here)
            def _():
                wg[rows] = final[core, rows]

            @pl.when(jnp.logical_not(here))
            def _():
                homeward(core, h).start()

    @pl.when(owns)
    def _():
        last_sum(1)
        last_sum(3)
        merge(odd, 2)
        last_sum(0)

    def near_first(h):
        total_y(zza, h)

        @pl.when(owns)
        def _():
            near_on(h)

        @pl.when(jnp.logical_not(owns))
        def _():
            start(far_z(h))

    def near_last(h):
        total_y(zzb, h)

        @pl.when(owns)
        def _():
            finish(h)

        @pl.when(jnp.logical_not(owns))
        def _():
            near_on(h)

    near_first(0)

    rows_t = xin

    @pl.when(s == 0)
    def _():
        rows_t[...] = gt[...]
        gates_ref[0] = gate_out[0:1]

    @pl.when(s == 1)
    def _():
        rows_back.wait_recv()
        gates_back.wait_recv()
        for i in range(2):
            packed = jnp.dot(xin[i], picks, preferred_element_type=F32)
            rows_t[i] = jnp.where(live, packed + pacc[i], 0.0).astype(BF16)
        gates_ref[0] = jnp.dot(gate_in[...], picks, preferred_element_type=F32).astype(BF16)[0:1]

    rows_ref[...] = (
        contract(fold[0], rows_t[0], 0, 0) + contract(fold[1], rows_t[1], 0, 0)
    ).astype(BF16)

    near_last(0)
    near_first(1)

    @pl.when(owns)
    def _():
        total_y(odd, 2)
        finish(2)

    near_last(1)

    total = q[x * 2 + c].astype(F32)
    for step in range(1, 4):
        xx = turn(x, step)
        send(qb.at[xx], qb.at[xx], os_.at[0], or_.at[xx], east).wait_recv()
        total = total + qb[xx].astype(F32)
    cgrad_ref[0, 0] = total.astype(BF16)

    @pl.when(jnp.logical_not(stays))
    def _():
        for h in range(3):
            rows = wg.at[pl.ds(START[h], SIZE[h])]
            send(rows, rows, ps.at[0, h], pr.at[h], holder).wait_recv()

    wgrad_ref[0] = wg[pl.ds(0, SLAB)]

    def left_already(copies):
        for copy in copies:
            copy.wait_send()

    @pl.when(owns)
    def _():
        for h in range(3):
            for core in range(2):
                @pl.when(jnp.logical_not(jnp.logical_and(diagonal, c == core)))
                def _():
                    homeward(core, h).wait_send()
        for h in range(2):
            left_already(along_z(h))
        left_already(along_y(zz1, 0, 2) + beyond_y(zz1, 0, 2))
        left_already(halves(odd, 2) + ways(odd, 2))
        for step in range(4):
            left_already(last_z(step))

    @pl.when(jnp.logical_not(owns))
    def _():
        for h in range(2):
            left_already(far_z(h))
        for step in range(4):
            left_already(last_far(step))

    def one_way(onward_way, near_way):
        for h in range(2):
            onward(h)[onward_way].wait_send()
            near_z(h)[near_way].wait_send()
        for step in range(4):
            last_onward(step)[onward_way].wait_send()
            last_near(step)[near_way].wait_send()

    @pl.when(from_left)
    def _():
        one_way(0, 1)

    @pl.when(jnp.logical_not(from_left))
    def _():
        one_way(1, 0)

    for h in range(2):
        for zz, u in ((zz1, 0), (zz2, 1)):
            left_already(along_y(zz, u, h) + beyond_y(zz, u, h) + halves(zz, h) + ways(zz, h))

    @pl.when(jnp.logical_not(stays))
    def _():
        to_holder(2).wait_send()

    for copy in always:
        copy.wait_send()
    for step in range(4):
        to_sibling(turn(x, step)).wait_send()
        if step:
            to_column(turn(x, step)).wait_send()

    @pl.when(s == 0)
    def _():
        rows_back.wait_send()
        gates_back.wait_send()

    @pl.when(s == 1)
    def _():
        rows_in.wait_send()


def call(*operands):
    dma = pltpu.SemaphoreType.DMA
    vmem = pl.BlockSpec(memory_space=pltpu.VMEM)

    def block(*lead, kind=BF16):
        return pltpu.VMEM((*lead, PAD, LEN), kind)

    return pl.pallas_call(
        kernel,
        name="relay",
        out_shape=(
            jax.ShapeDtypeStruct((COLS, LEN), BF16),
            jax.ShapeDtypeStruct((1, 1, LEN), BF16),
            jax.ShapeDtypeStruct((1, 1, LEN, INNER_DEV), BF16),
            jax.ShapeDtypeStruct((1, SLAB, INNER_DEV), BF16),
        ),
        in_specs=[vmem] * 4 + [pl.BlockSpec(memory_space=pltpu.SMEM), vmem],
        out_specs=(vmem,) * 4,
        scratch_shapes=[
            block(),
            block(16),
            pltpu.VMEM((8, LEN, INNER_DEV), BF16),
            block(2),
            pltpu.VMEM((2, PAD, 1), F32),
            block(2, kind=F32),
            block(2),
            block(2),
            block(2),
            pltpu.VMEM((8, LEN), F32),
            pltpu.VMEM((8, 8, LEN), F32),
            pltpu.VMEM((16, LEN), BF16),
            pltpu.VMEM((16, LEN), BF16),
            block(2),
            block(16),
            block(2, 2),
            block(8),
            block(2),
            block(4),
            pltpu.VMEM((8, SIZE[2], LEN), BF16),
            pltpu.VMEM((16, SIZE[2], LEN), BF16),
            block(4),
            block(2),
            block(),
            pltpu.VMEM((8, LEN, INNER_DEV), BF16),
            pltpu.VMEM((4, LEN, INNER_DEV), BF16),
            pltpu.VMEM((4, LEN, INNER_DEV), BF16),
            dma((12, 3)), dma((16, 3)), dma((3, 3)), dma((3,)), dma((8,)), dma((8, 2)), dma((4,)),
            dma((7,)), dma((7,)), dma((2, 2, 3)), dma((2, 2, 3)), dma((2, 2, 3)), dma((2, 2, 3)),
            dma((4, 2)), dma((4, 2)), dma((4,)), dma((4,)), dma((4,)), dma((4,)),
            dma((3, 4)), dma((4, 4)), dma((4, 4)),
            pltpu.SemaphoreType.REGULAR,
        ],
        compiler_params=pltpu.CompilerParams(
            collective_id=0, has_side_effects=True, vmem_limit_bytes=56 * 2**20
        ),
    )(*operands)


def hand_on_kernel(*refs):
    for source, target in zip(refs[:4], refs[4:]):
        target[...] = source[...]


def hand_on(*results):
    vmem = pl.BlockSpec(memory_space=pltpu.VMEM)
    return pl.pallas_call(
        hand_on_kernel,
        name="hand_on",
        out_shape=tuple(jax.ShapeDtypeStruct(v.shape, v.dtype) for v in results),
        in_specs=[vmem] * 4,
        out_specs=(vmem,) * 4,
    )(*results)


def per_device(byte_rows, context, weight, keep_list, counts, gate_vector):
    results = call(
        byte_rows[0, 0].T, context, weight, keep_list, counts, gate_vector
    )
    rows, gates, context_grad, weight_grad = hand_on(*results)
    return rows.T[None, None], gates, context_grad, weight_grad


def solution(mesh):
    placed = (
        P("section", "dp", None, "tensor"),
        P("section", "dp", None, "tensor"),
        P("section", "dp", "tensor"),
        P("dp", None),
        P("dp"),
        P("tensor"),
    )
    return jax.shard_map(
        per_device,
        mesh=mesh,
        in_specs=placed,
        out_specs=(
            P("section", "dp", None, "tensor"),
            P("section", "dp", None),
            P("section", "dp", None, "tensor"),
            P("section", "dp", "tensor"),
        ),
        check_vma=False,
    )
```

```python
import jax
import jax.numpy as jnp
from jax import lax
from jax.experimental import pallas as pl
from jax.experimental.pallas import tpu as pltpu
from jax.sharding import PartitionSpec as P

D = 4672
SLAB = 292
PAD = 304
START, SIZE = (0, 128, 240), (128, 112, 64)
COLS = 2 * SLAB
LEN = 512
INNER_DEV = 512
EPSILON = 1e-06
SHARPNESS = 30.0

MESH = pl.DeviceIdType.MESH
F32 = jnp.float32
BF16 = jnp.bfloat16


def turn(i, step):
    return lax.rem(i + step, 4)


def send(src, dst, send_sem, recv_sem, to):
    return pltpu.make_async_remote_copy(
        src_ref=src,
        dst_ref=dst,
        send_sem=send_sem,
        recv_sem=recv_sem,
        device_id=to,
        device_id_type=MESH,
    )


def contract(a, b, axis_a, axis_b):
    return lax.dot_general(
        a, b, (((axis_a,), (axis_b,)), ((), ())), preferred_element_type=F32
    )


def kernel(
    byte_ref, ctx_ref, w_ref, keep_ref, counts_ref, g_ref,
    rows_ref, gates_ref, cgrad_ref, wgrad_ref,
    stage, wf, cf, bt, gcol, pacc, spread, e_ref, gt, st_out, st_in, gate_out, gate_in, xin,
    wp, yh, yr, zh, zr, zhb, zrb, base, final, wg, q, qa, qb,
    ws, wr, ps, pr, cs_, cr, xs, ss, sr, hs, hr, fs, fr, zs, zrs, qs, qr, os_, or_, bs, vs, vr, ready,
):
    s = lax.axis_index("section")
    d = lax.axis_index("dp")
    t = lax.axis_index("tensor")
    y, z, x, c = lax.div(d, 4), lax.rem(d, 4), lax.div(t, 2), lax.rem(t, 2)

    def device(yy, zz, xx, cc):
        return (s, yy * 4 + zz, xx * 2 + cc)

    up, down = device(turn(y, 1), z, x, c), device(turn(y, 3), z, x, c)
    right, left = device(y, turn(z, 1), x, c), device(y, turn(z, 3), x, c)
    east, west = device(y, z, turn(x, 1), c), device(y, z, turn(x, 3), c)
    sibling = device(y, z, x, 1 - c)
    partner = (1 - s, d, t)
    team = [(s, d, lax.rem(t + j, 8)) for j in range(1, 8)]
    holder = device(x, z, y, lax.div(z, 2))
    owns = lax.div(z, 2) == c
    diagonal = x == y
    stays = jnp.logical_and(diagonal, owns)

    barrier = pltpu.get_barrier_semaphore()
    hello = [up, down, right, left, partner] + team
    for peer in hello:
        pl.semaphore_signal(barrier, inc=1, device_id=peer, device_id_type=MESH)

    @pl.when(jnp.logical_not(stays))
    def _():
        pl.semaphore_signal(barrier, inc=1, device_id=holder, device_id_type=MESH)

    for core in range(2):
        @pl.when(jnp.logical_and(owns, jnp.logical_not(jnp.logical_and(diagonal, c == core))))
        def _():
            pl.semaphore_signal(
                barrier, inc=1, device_id=device(x, z, y, core), device_id_type=MESH
            )

    stage[pl.ds(PAD - 16, 16)] = jnp.zeros((16, INNER_DEV), BF16)
    stage[pl.ds(0, SLAB)] = w_ref[0]
    cf[t] = ctx_ref[0, 0]
    fold = []
    for i in range(2):
        row = lax.broadcasted_iota(jnp.int32, (PAD, COLS), 0)
        col = lax.broadcasted_iota(jnp.int32, (PAD, COLS), 1)
        hit = jnp.logical_and(col == row + i * SLAB, row < SLAB)
        fold.append(jnp.where(hit, 1.0, 0.0).astype(BF16))
    for i in range(2):
        bt[i] = jnp.dot(fold[i], byte_ref[...], preferred_element_type=F32).astype(BF16)

    greeted = (
        len(hello)
        + jnp.where(stays, 0, 1)
        + jnp.where(owns, jnp.where(diagonal, 1, 2), 0)
    )
    pl.semaphore_wait(barrier, greeted)

    def unit(yy, zz):
        return yy * 4 + zz * 2

    def pair(ref, n, h):
        return ref.at[pl.ds(n, 2), pl.ds(START[h], SIZE[h])]

    def one(ref, n, h):
        return ref.at[n, pl.ds(START[h], SIZE[h])]

    always = []

    def go(copy):
        copy.start()
        always.append(copy)

    def start(copies):
        for copy in copies:
            copy.start()

    home = x * 4 + lax.rem(z, 2) * 2 + c

    def to_holder(h):
        rows = stage.at[pl.ds(START[h], SIZE[h])]
        return send(rows, one(wf, home, h), ps.at[2, h], wr.at[home, h], holder)

    @pl.when(stays)
    def _():
        wf[home] = stage[...]

    @pl.when(jnp.logical_not(stays))
    def _():
        to_holder(0).start()

    rows_in = send(bt, xin, xs.at[0], xs.at[1], partner)
    rows_back = send(e_ref, xin, xs.at[0], xs.at[1], partner)
    gates_back = send(gate_out, gate_in, xs.at[2], xs.at[3], partner)

    @pl.when(s == 1)
    def _():
        rows_in.start()

    odd = lax.rem(z, 2)
    zz1 = jnp.where(owns, odd, 1 - odd)
    zz2 = 1 - zz1
    near = 1 - odd
    from_left = owns == (odd == 1)
    half = LEN // 2

    def context_out():
        for i, to in enumerate((east, west, sibling)):
            go(send(ctx_ref.at[0, 0], cf.at[t], cs_.at[i], cr.at[t, 0], to))

    def wait_context(it, part):
        rows = cf.at[it]
        if part is not None:
            rows = cf.at[it, pl.ds(part * half, half)]
        send(rows, rows, cs_.at[0], cr.at[it, part or 0], east).wait_recv()

    def context_on():
        for i, (xx, to) in enumerate(((turn(x, 3), east), (turn(x, 1), west))):
            it = xx * 2 + c
            wait_context(it, None)
            rows = cf.at[it, pl.ds(i * half, half)]
            go(send(rows, rows, cs_.at[3 + i], cr.at[it, i], to))
            go(send(cf.at[it], cf.at[it], cs_.at[5 + i], cr.at[it, 0], sibling))

    def context_last():
        it = turn(x, 2) * 2 + c
        wait_context(it, 0)
        wait_context(it, 1)
        go(send(cf.at[it], cf.at[it], cs_.at[7], cr.at[it, 0], sibling))
        for xx in range(4):
            wait_context(xx * 2 + 1 - c, None)

    def arrived(n, h):
        send(pair(wf, n, h), pair(wf, n, h), ws.at[0, h], wr.at[n, h], up).wait_recv()

    def arrived_block(n, h):
        send(one(wf, n, h), one(wf, n, h), ws.at[0, h], wr.at[n, h], up).wait_recv()

    def pass_pair(n, h, i, to):
        return send(pair(wf, n, h), pair(wf, n, h), ws.at[i, h], wr.at[n, h], to)

    def pass_one(n, h, i, to):
        return send(one(wf, n, h), one(wf, n, h), ws.at[i, h], wr.at[n, h], to)

    def along_y(zz, u, h):
        n = unit(y, zz)
        return pass_pair(n, h, 4 + 4 * u, up), pass_pair(n, h, 5 + 4 * u, down)

    def beyond_y(zz, u, h):
        n, m = unit(turn(y, 3), zz), unit(turn(y, 1), zz) + 1
        return pass_one(n, h, 6 + 4 * u, up), pass_one(m, h, 7 + 4 * u, down)

    def on_along_y(zz, u, h):
        ahead, back = beyond_y(zz, u, h)
        arrived(unit(turn(y, 3), zz), h)
        ahead.start()
        arrived(unit(turn(y, 1), zz), h)
        back.start()

    def along_z(h):
        n = unit(y, odd)
        return pass_pair(n, h, 1, right), pass_pair(n, h, 2, left)

    def arrived_far(yy, zz, h):
        n = unit(yy, zz)
        arrived_block(n, h)
        arrived_block(n + 1, h)

    def onward(h):
        n = unit(y, near)
        return pass_one(n, h, 3, right), pass_one(n + 1, h, 3, left)

    def on_along_z(h):
        arrived(unit(y, near), h)

        @pl.when(from_left)
        def _():
            onward(h)[0].start()

        @pl.when(jnp.logical_not(from_left))
        def _():
            onward(h)[1].start()

    def last_z(step):
        n = unit(turn(y, step), odd)
        return (
            send(pair(wf, n, 2), pair(wf, n, 2), bs.at[0, step], wr.at[n, 2], right),
            send(pair(wf, n, 2), pair(wf, n, 2), bs.at[1, step], wr.at[n, 2], left),
        )

    def last_onward(step):
        n = unit(turn(y, step), near)
        m = n + 1
        return (
            send(one(wf, n, 2), one(wf, n, 2), bs.at[2, step], wr.at[n, 2], right),
            send(one(wf, m, 2), one(wf, m, 2), bs.at[2, step], wr.at[m, 2], left),
        )

    def last_on_along_z(step):
        arrived(unit(turn(y, step), near), 2)

        @pl.when(from_left)
        def _():
            last_onward(step)[0].start()

        @pl.when(jnp.logical_not(from_left))
        def _():
            last_onward(step)[1].start()

    def project(yy, zz):
        n = unit(yy, zz)
        pacc[zz] += contract(wf[n], cf[yy * 2], 1, 1) + contract(wf[n + 1], cf[yy * 2 + 1], 1, 1)

    pacc[...] = jnp.zeros_like(pacc)

    @pl.when(jnp.logical_not(stays))
    def _():
        for h in range(2):
            to_holder(h).wait_send()
            to_holder(h + 1).start()

    @pl.when(owns)
    def _():
        for h in range(3):
            for core in range(2):
                @pl.when(jnp.logical_not(jnp.logical_and(diagonal, c == core)))
                def _():
                    arrived_block(unit(y, zz1) + core, h)
            if h < 2:
                start(along_z(h))
            start(along_y(zz1, 0, h))
        pl.semaphore_signal(ready, inc=1, device_id=sibling, device_id_type=MESH)

    @pl.when(jnp.logical_not(owns))
    def _():
        on_along_z(0)
        start(along_y(zz1, 0, 0))
        pl.semaphore_wait(ready, 1)

    context_out()

    @pl.when(owns)
    def _():
        for h in range(2):
            on_along_y(zz1, 0, h)
            on_along_z(h)
            start(along_y(zz2, 1, h))
        start(last_z(0))
        on_along_y(zz1, 0, 2)
        start(last_z(1))
        start(last_z(3))
        arrived_far(turn(y, 2), zz1, 2)
        start(last_z(2))

    @pl.when(jnp.logical_not(owns))
    def _():
        arrived_far(y, zz2, 0)
        start(along_y(zz2, 1, 0))
        on_along_z(1)
        start(along_y(zz1, 0, 1))
        arrived_far(y, zz2, 1)
        start(along_y(zz2, 1, 1))

    last_on_along_z(0)
    context_on()

    @pl.when(owns)
    def _():
        on_along_y(zz2, 1, 0)

    @pl.when(jnp.logical_not(owns))
    def _():
        on_along_y(zz1, 0, 0)

    last_on_along_z(1)
    last_on_along_z(3)

    @pl.when(owns)
    def _():
        on_along_y(zz2, 1, 1)

    @pl.when(jnp.logical_not(owns))
    def _():
        on_along_y(zz2, 1, 0)
        on_along_y(zz1, 0, 1)

    last_on_along_z(2)
    context_last()

    @pl.when(jnp.logical_not(owns))
    def _():
        for step in (0, 1, 3):
            arrived_far(turn(y, step), odd, 2)

    pick = jnp.where(
        lax.broadcasted_iota(jnp.int32, (1, LEN), 1) < counts_ref[0], keep_ref[...], -1
    )
    live = pick >= 0
    place_of = lax.broadcasted_iota(jnp.int32, (LEN, LEN), 0)
    picks = jnp.where(pick == place_of, 1.0, 0.0).astype(BF16)

    project(y, zz1)
    project(y, zz2)

    @pl.when(jnp.logical_not(owns))
    def _():
        on_along_y(zz2, 1, 1)

    project(turn(y, 1), zz1)
    project(turn(y, 3), zz1)
    for h in range(2):
        arrived_far(turn(y, 2), zz1, h)
    project(turn(y, 1), zz2)
    project(turn(y, 3), zz2)

    @pl.when(jnp.logical_not(owns))
    def _():
        arrived_far(turn(y, 2), odd, 2)

    project(turn(y, 2), zz1)

    g = g_ref[...].reshape(1, COLS)
    first = g.astype(BF16)
    rest = g - first.astype(F32)
    second = rest.astype(BF16)
    third = (rest - second.astype(F32)).astype(BF16)
    for i in range(2):
        terms = [contract(fold[i], jnp.broadcast_to(v, (16, COLS)), 1, 1) for v in (first, second, third)]
        gcol[i] = (terms[0] + terms[1] + terms[2])[:, 0:1]

    arrived_far(turn(y, 2), zz2, 0)
    arrived_far(turn(y, 2), zz2, 1)
    project(turn(y, 2), zz2)

    @pl.when(s == 0)
    def _():
        st_out[...] = jnp.zeros_like(st_out)
        for i in range(2):
            e = (bt[i].astype(F32) + pacc[i]).astype(BF16)
            e_ref[i] = e
            e = e.astype(F32)
            st_out[0:1] += jnp.sum(e * e, axis=0, keepdims=True)
            st_out[1:2] += jnp.sum(e * gcol[i], axis=0, keepdims=True)
        st_in[t] = st_out[...]
        stats = [
            send(st_out, st_in.at[t], ss.at[j], sr.at[j], peer) for j, peer in enumerate(team)
        ]
        for copy in stats:
            copy.start()
        rows_back.start()
        rows_in.wait_recv()
        for i in range(2):
            spread[i] = contract(xin[i], picks, 1, 1).astype(BF16)
        for copy in stats:
            copy.wait()
        sums = st_in[0]
        for j in range(1, 8):
            sums = sums + st_in[j]
        inverse = lax.rsqrt(sums[0:1] / D + EPSILON)
        score = inverse * sums[1:2]
        squashed = jax.nn.sigmoid(score)
        gate = (-SHARPNESS * squashed).astype(BF16)
        gate_out[...] = jnp.broadcast_to(gate, gate_out.shape)
        gates_back.start()
        slope = -SHARPNESS * squashed * (1.0 - squashed)
        pull = score * inverse * inverse / D
        for i in range(2):
            gate_part = slope * (inverse * gcol[i] - pull * e_ref[i].astype(F32))
            gt[i] = (spread[i].astype(F32) + gate_part).astype(BF16)

    @pl.when(s == 1)
    def _():
        for i in range(2):
            rows = bt[i]
            gt[i] = jnp.where(live, rows, jnp.zeros_like(rows))

    zza = jnp.where(owns, near, odd)
    zzb = 1 - zza

    def products(yy, zz):
        n = unit(yy, zz)
        for core in range(2):
            wp[n + core] = jnp.dot(
                gt[zz], cf[yy * 2 + core], preferred_element_type=F32
            ).astype(BF16)

    def halves(zz, h):
        n = unit(turn(y, 2), zz)
        return (
            send(one(wp, n, h), yh.at[0, zz, pl.ds(START[h], SIZE[h])], hs.at[0, zz, h], hr.at[0, zz, h], up),
            send(one(wp, n + 1, h), yh.at[1, zz, pl.ds(START[h], SIZE[h])], hs.at[1, zz, h], hr.at[1, zz, h], down),
        )

    def ways(zz, h):
        n, m = unit(turn(y, 1), zz), unit(turn(y, 3), zz)
        return (
            send(pair(wp, n, h), pair(yr, zz * 2, h), fs.at[0, zz, h], fr.at[0, zz, h], up),
            send(pair(wp, m, h), pair(yr, 4 + zz * 2, h), fs.at[1, zz, h], fr.at[1, zz, h], down),
        )

    def merge(zz, h):
        rows = pl.ds(START[h], SIZE[h])
        to_up, to_down = halves(zz, h)
        on_up, on_down = ways(zz, h)
        n = unit(turn(y, 1), zz)
        to_up.wait_recv()
        wp[n, rows] = (wp[n, rows].astype(F32) + yh[0, zz, rows].astype(F32)).astype(BF16)
        on_up.start()
        n = unit(turn(y, 3), zz) + 1
        to_down.wait_recv()
        wp[n, rows] = (wp[n, rows].astype(F32) + yh[1, zz, rows].astype(F32)).astype(BF16)
        on_down.start()

    rows2 = pl.ds(START[2], SIZE[2])

    def last_far(step):
        n = unit(turn(y, step), odd)
        return (
            send(one(wp, n, 2), zhb.at[step * 2], vs.at[0, step], vr.at[0, step], right),
            send(one(wp, n + 1, 2), zhb.at[step * 2 + 1], vs.at[1, step], vr.at[1, step], left),
        )

    def last_near(step):
        n = unit(turn(y, step), near)
        return (
            send(
                pair(wp, n, 2), zrb.at[pl.ds(step * 4, 2)],
                vs.at[2, step], vr.at[2, step], right,
            ),
            send(
                pair(wp, n, 2), zrb.at[pl.ds(step * 4 + 2, 2)],
                vs.at[3, step], vr.at[3, step], left,
            ),
        )

    def last_far_out(*steps):
        @pl.when(jnp.logical_not(owns))
        def _():
            for step in steps:
                start(last_far(step))

    def last_near_on(step):
        def add(way):
            last_far(step)[way].wait_recv()
            n = unit(turn(y, step), near) + way
            wp[n, rows2] = (wp[n, rows2].astype(F32) + zhb[step * 2 + way].astype(F32)).astype(BF16)
            last_near(step)[way].start()

        @pl.when(from_left)
        def _():
            add(1)

        @pl.when(jnp.logical_not(from_left))
        def _():
            add(0)

    def last_sum(step):
        for copy in last_near(step):
            copy.wait_recv()
        for core in range(2):
            n = unit(turn(y, step), odd) + core
            total = wp[n, rows2].astype(F32)
            for way in range(2):
                total = total + zrb[step * 4 + way * 2 + core].astype(F32)
            wp[n, rows2] = total.astype(BF16)

    products(turn(y, 2), zza)
    start(halves(zza, 0))
    last_far_out(2)
    products(turn(y, 2), zzb)
    start(halves(zzb, 0))
    products(turn(y, 1), zza)
    products(turn(y, 3), zza)
    last_far_out(1, 3)
    merge(zza, 0)
    start(halves(zza, 1))
    start(halves(zzb, 1))
    products(turn(y, 1), zzb)
    products(turn(y, 3), zzb)
    merge(zzb, 0)
    products(y, zza)
    last_far_out(0)
    products(y, zzb)
    last_near_on(2)
    last_near_on(1)
    merge(zza, 1)
    last_near_on(3)
    merge(zzb, 1)
    last_near_on(0)

    @pl.when(owns)
    def _():
        last_sum(2)
        start(halves(odd, 2))

    def to_sibling(xx):
        return send(q.at[xx * 2 + 1 - c], qa.at[xx], qs.at[xx], qr.at[xx], sibling)

    def to_column(xx):
        return send(q.at[xx * 2 + c], qb.at[x], os_.at[xx], or_.at[x], device(y, z, xx, c))

    def context_part(it):
        n = lax.div(it, 2) * 4 + lax.rem(it, 2)
        return contract(gt[0], wf[n], 0, 0) + contract(gt[1], wf[n + 2], 0, 0)

    @pl.loop(0, 4)
    def _(j):
        xx = turn(x, j + 1)
        q[xx * 2 + 1 - c] = context_part(xx * 2 + 1 - c).astype(BF16)
        to_sibling(xx).start()

    @pl.loop(0, 4)
    def _(j):
        xx = turn(x, j + 1)
        part = context_part(xx * 2 + c)
        to_sibling(xx).wait_recv()
        q[xx * 2 + c] = (part + qa[xx].astype(F32)).astype(BF16)

        @pl.when(j < 3)
        def _():
            to_column(xx).start()

    def far_z(h):
        return (
            send(one(base, odd * 2, h), one(zh, 0, h), zs.at[0, h], zrs.at[0, h], right),
            send(one(base, odd * 2 + 1, h), one(zh, 1, h), zs.at[1, h], zrs.at[1, h], left),
        )

    def near_z(h):
        return (
            send(pair(base, near * 2, h), pair(zr, 0, h), zs.at[2, h], zrs.at[2, h], right),
            send(pair(base, near * 2, h), pair(zr, 2, h), zs.at[3, h], zrs.at[3, h], left),
        )

    def total_y(zz, h):
        rows = pl.ds(START[h], SIZE[h])
        for copy in ways(zz, h):
            copy.wait_recv()
        for core in range(2):
            total = wp[unit(y, zz) + core, rows].astype(F32)
            for way in range(2):
                total = total + yr[way * 4 + zz * 2 + core, rows].astype(F32)
            base[zz * 2 + core, rows] = total.astype(BF16)

    def near_on(h):
        rows = pl.ds(START[h], SIZE[h])

        def add(way):
            far_z(h)[way].wait_recv()
            n = near * 2 + way
            base[n, rows] = (base[n, rows].astype(F32) + zh[way, rows].astype(F32)).astype(BF16)
            near_z(h)[way].start()

        @pl.when(from_left)
        def _():
            add(1)

        @pl.when(jnp.logical_not(from_left))
        def _():
            add(0)

    def homeward(core, h):
        rows = wg.at[pl.ds(START[h], SIZE[h])]
        return send(one(final, core, h), rows, ps.at[core, h], pr.at[h], device(x, z, y, core))

    def finish(h):
        rows = pl.ds(START[h], SIZE[h])
        if h < 2:
            near_z(h)[0].wait_recv()
            near_z(h)[1].wait_recv()
        for core in range(2):
            total = base[odd * 2 + core, rows].astype(F32)
            for way in range(2 if h < 2 else 0):
                total = total + zr[way * 2 + core, rows].astype(F32)
            final[core, rows] = total.astype(BF16)
            here = jnp.logical_and(diagonal, c == core)

            @pl.when(here)
            def _():
                wg[rows] = final[core, rows]

            @pl.when(jnp.logical_not(here))
            def _():
                homeward(core, h).start()

    @pl.when(owns)
    def _():
        last_sum(1)
        last_sum(3)
        merge(odd, 2)
        last_sum(0)

    def near_first(h):
        total_y(zza, h)

        @pl.when(owns)
        def _():
            near_on(h)

        @pl.when(jnp.logical_not(owns))
        def _():
            start(far_z(h))

    def near_last(h):
        total_y(zzb, h)

        @pl.when(owns)
        def _():
            finish(h)

        @pl.when(jnp.logical_not(owns))
        def _():
            near_on(h)

    near_first(0)

    near_last(0)
    near_first(1)

    @pl.when(owns)
    def _():
        total_y(odd, 2)
        finish(2)

    near_last(1)

    rows_t = xin

    @pl.when(s == 0)
    def _():
        rows_t[...] = gt[...]
        gates_ref[0] = gate_out[0:1]

    @pl.when(s == 1)
    def _():
        rows_back.wait_recv()
        gates_back.wait_recv()
        for i in range(2):
            packed = jnp.dot(xin[i], picks, preferred_element_type=F32)
            rows_t[i] = jnp.where(live, packed + pacc[i], 0.0).astype(BF16)
        gates_ref[0] = jnp.dot(gate_in[...], picks, preferred_element_type=F32).astype(BF16)[0:1]

    rows_ref[...] = (
        contract(fold[0], rows_t[0], 0, 0) + contract(fold[1], rows_t[1], 0, 0)
    ).astype(BF16)

    total = q[x * 2 + c].astype(F32)
    for step in range(1, 4):
        xx = turn(x, step)
        send(qb.at[xx], qb.at[xx], os_.at[0], or_.at[xx], east).wait_recv()
        total = total + qb[xx].astype(F32)
    cgrad_ref[0, 0] = total.astype(BF16)

    @pl.when(jnp.logical_not(stays))
    def _():
        for h in range(3):
            rows = wg.at[pl.ds(START[h], SIZE[h])]
            send(rows, rows, ps.at[0, h], pr.at[h], holder).wait_recv()

    wgrad_ref[0] = wg[pl.ds(0, SLAB)]

    def left_already(copies):
        for copy in copies:
            copy.wait_send()

    @pl.when(owns)
    def _():
        for h in range(3):
            for core in range(2):
                @pl.when(jnp.logical_not(jnp.logical_and(diagonal, c == core)))
                def _():
                    homeward(core, h).wait_send()
        for h in range(2):
            left_already(along_z(h))
        left_already(along_y(zz1, 0, 2) + beyond_y(zz1, 0, 2))
        left_already(halves(odd, 2) + ways(odd, 2))
        for step in range(4):
            left_already(last_z(step))

    @pl.when(jnp.logical_not(owns))
    def _():
        for h in range(2):
            left_already(far_z(h))
        for step in range(4):
            left_already(last_far(step))

    def one_way(onward_way, near_way):
        for h in range(2):
            onward(h)[onward_way].wait_send()
            near_z(h)[near_way].wait_send()
        for step in range(4):
            last_onward(step)[onward_way].wait_send()
            last_near(step)[near_way].wait_send()

    @pl.when(from_left)
    def _():
        one_way(0, 1)

    @pl.when(jnp.logical_not(from_left))
    def _():
        one_way(1, 0)

    for h in range(2):
        for zz, u in ((zz1, 0), (zz2, 1)):
            left_already(along_y(zz, u, h) + beyond_y(zz, u, h) + halves(zz, h) + ways(zz, h))

    @pl.when(jnp.logical_not(stays))
    def _():
        to_holder(2).wait_send()

    for copy in always:
        copy.wait_send()
    for step in range(4):
        to_sibling(turn(x, step)).wait_send()
        if step:
            to_column(turn(x, step)).wait_send()

    @pl.when(s == 0)
    def _():
        rows_back.wait_send()
        gates_back.wait_send()

    @pl.when(s == 1)
    def _():
        rows_in.wait_send()


def call(*operands):
    dma = pltpu.SemaphoreType.DMA
    vmem = pl.BlockSpec(memory_space=pltpu.VMEM)

    def block(*lead, kind=BF16):
        return pltpu.VMEM((*lead, PAD, LEN), kind)

    return pl.pallas_call(
        kernel,
        name="relay",
        out_shape=(
            jax.ShapeDtypeStruct((COLS, LEN), BF16),
            jax.ShapeDtypeStruct((1, 1, LEN), BF16),
            jax.ShapeDtypeStruct((1, 1, LEN, INNER_DEV), BF16),
            jax.ShapeDtypeStruct((1, SLAB, INNER_DEV), BF16),
        ),
        in_specs=[vmem] * 4 + [pl.BlockSpec(memory_space=pltpu.SMEM), vmem],
        out_specs=(vmem,) * 4,
        scratch_shapes=[
            block(),
            block(16),
            pltpu.VMEM((8, LEN, INNER_DEV), BF16),
            block(2),
            pltpu.VMEM((2, PAD, 1), F32),
            block(2, kind=F32),
            block(2),
            block(2),
            block(2),
            pltpu.VMEM((8, LEN), F32),
            pltpu.VMEM((8, 8, LEN), F32),
            pltpu.VMEM((16, LEN), BF16),
            pltpu.VMEM((16, LEN), BF16),
            block(2),
            block(16),
            block(2, 2),
            block(8),
            block(2),
            block(4),
            pltpu.VMEM((8, SIZE[2], LEN), BF16),
            pltpu.VMEM((16, SIZE[2], LEN), BF16),
            block(4),
            block(2),
            block(),
            pltpu.VMEM((8, LEN, INNER_DEV), BF16),
            pltpu.VMEM((4, LEN, INNER_DEV), BF16),
            pltpu.VMEM((4, LEN, INNER_DEV), BF16),
            dma((12, 3)), dma((16, 3)), dma((3, 3)), dma((3,)), dma((8,)), dma((8, 2)), dma((4,)),
            dma((7,)), dma((7,)), dma((2, 2, 3)), dma((2, 2, 3)), dma((2, 2, 3)), dma((2, 2, 3)),
            dma((4, 2)), dma((4, 2)), dma((4,)), dma((4,)), dma((4,)), dma((4,)),
            dma((3, 4)), dma((4, 4)), dma((4, 4)),
            pltpu.SemaphoreType.REGULAR,
        ],
        compiler_params=pltpu.CompilerParams(
            collective_id=0, has_side_effects=True, vmem_limit_bytes=56 * 2**20
        ),
    )(*operands)


def hand_on_kernel(*refs):
    for source, target in zip(refs[:4], refs[4:]):
        target[...] = source[...]


def hand_on(*results):
    vmem = pl.BlockSpec(memory_space=pltpu.VMEM)
    return pl.pallas_call(
        hand_on_kernel,
        name="hand_on",
        out_shape=tuple(jax.ShapeDtypeStruct(v.shape, v.dtype) for v in results),
        in_specs=[vmem] * 4,
        out_specs=(vmem,) * 4,
    )(*results)


def per_device(byte_rows, context, weight, keep_list, counts, gate_vector):
    results = call(
        byte_rows[0, 0].T, context, weight, keep_list, counts, gate_vector
    )
    rows, gates, context_grad, weight_grad = hand_on(*results)
    return rows.T[None, None], gates, context_grad, weight_grad


def solution(mesh):
    placed = (
        P("section", "dp", None, "tensor"),
        P("section", "dp", None, "tensor"),
        P("section", "dp", "tensor"),
        P("dp", None),
        P("dp"),
        P("tensor"),
    )
    return jax.shard_map(
        per_device,
        mesh=mesh,
        in_specs=placed,
        out_specs=(
            P("section", "dp", None, "tensor"),
            P("section", "dp", None),
            P("section", "dp", None, "tensor"),
            P("section", "dp", "tensor"),
        ),
        check_vma=False,
    )
```
